32 devices in a mesh: groups: 2 (over y), row: 4 (over z), col: 2 (over x), rep: 2 (over core).
Axes of the slice: x: 2, y: 2, z: 4, core: 2. Of those that a mesh axis runs over, the one named last changes fastest.
Arguments:
- source_emb: bfloat16 [16384, 256], P(('groups', 'row')), parts along dimension 0, may hold values from -6 to 6
- target_emb: bfloat16 [8192, 256], P(('groups', 'col')), parts along dimension 0, may hold values from -6 to 6
- warm_start: float32 [8192], P(('groups', 'col')), parts along dimension 0, may hold values from -4 to 210
- source_weight: float32 [16384], P(('groups', 'row')), parts along dimension 0, may hold values from 1 to 10
- target_weight: float32 [8192], P(('groups', 'col')), parts along dimension 0, may hold values from 1 to 10
- source_bounds: int32 [18], P('groups'), parts along dimension 0, may hold values from 0 to 16, as said below
- target_bounds: int32 [10], P('groups'), parts along dimension 0, may hold values from 0 to 8, as said below
- kept_pairs: int32 [32, 2], P('groups'), parts along dimension 0, may hold values from 0 to 7, as said below
Outputs:
- grad_source: bfloat16 [16384, 256], P(('groups', 'row', 'col', 'rep')), parts along dimension 0
- grad_target: bfloat16 [8192, 256], P(('groups', 'col')), parts along dimension 0
The draws below stay inside these ranges and needn't reach their ends.
There are 2 independent parts, one for each index of `groups`. The reference program is written for one: setup_inputs(seed, part) draws one part's arguments, and reference() takes and returns one part's arrays. A program takes and returns all parts, laid end to end along the dimension named above; each array names one. Nothing has to cross between parts.
Inputs may be any that keep to these rules, and one draw needn't show every extreme that they name: Cluster k of the source cohort is tiles source_bounds[k] to source_bounds[k + 1] - 1; the bounds rise strictly from 0 to the end; each block of 4 tiles of one index of row holds exactly two clusters. Cluster k of the target cohort is tiles target_bounds[k] to target_bounds[k + 1] - 1; the bounds rise strictly from 0 to the end; each block of 4 tiles of one index of col holds exactly two clusters. `kept_pairs`: each pair of a source block and a target block holds exactly two listed pairs, which match its two source clusters one to one with its two target clusters; in some pair of blocks (3) * 3 + 1 tiles are kept, and in none more.
All inputs are finite; a program needn't handle non-finite values.
Results may differ from the reference program's by a relative error of at most 0.0042.
Values may be sent and summed in bfloat16 or wider, within the bound.
No kernel may reach another device: no remote copies, remote signals or barrier semaphores. Data moves between devices by JAX's collectives and lax.ppermute only.
A program may use at most 64 MiB of HBM per device.

```python
import math
import jax
import jax.numpy as jnp
from jax import lax

D = 256
TILE = 512
TS = 4
TT = 4
NS = 8192
NT = 4096
NPAIRS = 16
KCAP = 10
N_ROW = 4
N_COL = 2


def pattern(key):
    src_cut = jax.random.randint(jax.random.fold_in(key, 107), (N_ROW,), 1, TS)
    tgt_cut = jax.random.randint(jax.random.fold_in(key, 108), (N_COL,), 1, TT)
    flips = jax.random.randint(jax.random.fold_in(key, 109), (N_ROW, N_COL), 0, 2)
    forced_row = jax.random.randint(jax.random.fold_in(key, 105), (), 0, N_ROW)
    forced_col = jax.random.randint(jax.random.fold_in(key, 106), (), 0, N_COL)
    row_here = jnp.arange(N_ROW) == forced_row
    col_here = jnp.arange(N_COL) == forced_col
    src_cut = jnp.where(row_here, 1, src_cut)
    tgt_cut = jnp.where(col_here, 1, tgt_cut)
    flips = jnp.where(row_here[:, None] & col_here[None, :], 0, flips)
    return (src_cut, tgt_cut, flips)


def draw_source_bounds(key, part):
    src_cut, tgt_cut, flips = pattern(key)
    starts = jnp.arange(N_ROW, dtype=jnp.int32) * TS
    inner = starts + src_cut.astype(jnp.int32)
    bounds = jnp.stack([starts, inner], axis=1).reshape(-1)
    return jnp.concatenate([bounds, jnp.full((1,), N_ROW * TS, jnp.int32)]).astype(jnp.int32)


def draw_target_bounds(key, part):
    src_cut, tgt_cut, flips = pattern(key)
    starts = jnp.arange(N_COL, dtype=jnp.int32) * TT
    inner = starts + tgt_cut.astype(jnp.int32)
    bounds = jnp.stack([starts, inner], axis=1).reshape(-1)
    return jnp.concatenate([bounds, jnp.full((1,), N_COL * TT, jnp.int32)]).astype(jnp.int32)


def draw_kept_pairs(key, part):
    src_cut, tgt_cut, flips = pattern(key)
    key = jax.random.fold_in(key, 3)
    row_ids = jnp.broadcast_to(jnp.arange(N_ROW, dtype=jnp.int32)[:, None], (N_ROW, N_COL))
    col_ids = jnp.broadcast_to(jnp.arange(N_COL, dtype=jnp.int32)[None, :], (N_ROW, N_COL))
    flips = flips.astype(jnp.int32)
    first_pair = jnp.stack([2 * row_ids, 2 * col_ids + flips], axis=-1)
    second_pair = jnp.stack([2 * row_ids + 1, 2 * col_ids + 1 - flips], axis=-1)
    pairs = jnp.stack([first_pair, second_pair], axis=2).reshape(NPAIRS, 2)
    shuffle = jax.random.permutation(key, NPAIRS)
    return pairs[shuffle].astype(jnp.int32)


def draw_source_emb(key, part):
    key = jax.random.fold_in(key, 4)
    values = jax.random.truncated_normal(key, -6.0, 6.0, (NS, D), jnp.float32)
    return values.astype(jnp.bfloat16)


def draw_target_emb(key, part):
    key = jax.random.fold_in(key, 5)
    values = jax.random.truncated_normal(key, -6.0, 6.0, (NT, D), jnp.float32)
    return values.astype(jnp.bfloat16)


def draw_warm_start(key, part):
    key = jax.random.fold_in(key, 7)
    values = jax.random.truncated_normal(key, -4.0, 4.0, (NT,), jnp.float32)
    return values.astype(jnp.float32)


def steps_of(own_key, extent, pieces, smallest, top_value):
    gain = 1.0
    for axis_at, shards_of in pieces:
        heights = jax.random.uniform(jax.random.fold_in(jax.random.fold_in(own_key, 6), axis_at), (shards_of,), jnp.float32, smallest / len(pieces), top_value / len(pieces))
        gain = gain * jnp.repeat(jnp.exp(heights), extent[axis_at] // shards_of).reshape((-1,) + (1,) * (len(extent) - 1 - axis_at))
    return gain


def setup_inputs(seed: int = 0, part: int = 0) -> dict:
    arg_keys = jax.random.split(jax.random.key(seed), 9)
    own_keys = jax.random.split(jax.random.fold_in(arg_keys[8], part), 9)
    return {
        "source_emb": draw_source_emb(jax.random.fold_in(jax.random.fold_in(arg_keys[8], part), 71), part),
        "target_emb": draw_target_emb(jax.random.fold_in(jax.random.fold_in(arg_keys[8], part), 71), part),
        "warm_start": draw_warm_start(jax.random.fold_in(jax.random.fold_in(arg_keys[8], part), 71), part),
        "source_weight": jnp.clip(jnp.exp(math.log(10.0) - 2.3025851 * jax.random.uniform(own_keys[3], (NS,), jnp.float32) ** steps_of(own_keys[3], (NS,), ((0, 4),), -0.2, 0.2)), 1.0, 10.0),
        "target_weight": jnp.clip(jnp.exp(math.log(10.0) - 2.3025851 * jax.random.uniform(own_keys[4], (NT,), jnp.float32) ** steps_of(own_keys[4], (NT,), ((0, 2),), -0.2, 0.2)), 1.0, 10.0),
        "source_bounds": draw_source_bounds(jax.random.fold_in(jax.random.fold_in(arg_keys[8], part), 71), part),
        "target_bounds": draw_target_bounds(jax.random.fold_in(jax.random.fold_in(arg_keys[8], part), 71), part),
        "kept_pairs": draw_kept_pairs(jax.random.fold_in(jax.random.fold_in(arg_keys[8], part), 71), part),
    }


temper = 1.0
sentinel = -1e+30

def tile_layout(source_bounds, target_bounds, kept_pairs):
    src_count = N_ROW * TS
    tgt_count = N_COL * TT
    src_ids = jnp.arange(src_count, dtype=jnp.int32)
    tgt_ids = jnp.arange(tgt_count, dtype=jnp.int32)
    src_cluster = lax.optimization_barrier(jnp.sum((source_bounds[1:-1][None, :] <= src_ids[:, None]).astype(jnp.int32), axis=1)).astype(jnp.int32)
    tgt_cluster = lax.optimization_barrier(jnp.sum((target_bounds[1:-1][None, :] <= tgt_ids[:, None]).astype(jnp.int32), axis=1)).astype(jnp.int32)
    matches = (kept_pairs[:, 0][None, None, :] == src_cluster[:, None, None]) & (kept_pairs[:, 1][None, None, :] == tgt_cluster[None, :, None])
    marks = jnp.any(matches, axis=2).astype(jnp.int32)
    blocks = marks.reshape(N_ROW, TS, N_COL, TT).transpose(0, 2, 1, 3).reshape(N_ROW, N_COL, TS * TT)
    order_rank = (jnp.cumsum(blocks, axis=2) - 1).astype(jnp.int32)
    slot_ids = jnp.arange(KCAP, dtype=jnp.int32)
    chosen = (blocks[:, :, None, :] == 1) & (order_rank[:, :, None, :] == slot_ids[None, None, :, None])
    occupied = jnp.any(chosen, axis=3)
    flat_index = lax.optimization_barrier(jnp.sum(chosen.astype(jnp.int32) * jnp.arange(TS * TT, dtype=jnp.int32), axis=3)).astype(jnp.int32)
    src_tile = jnp.arange(N_ROW, dtype=jnp.int32)[:, None, None] * TS + flat_index // TT
    tgt_tile = jnp.arange(N_COL, dtype=jnp.int32)[None, :, None] * TT + flat_index % TT
    return (src_tile.reshape(-1), tgt_tile.reshape(-1), occupied.reshape(-1))

def reference(source_emb, target_emb, warm_start, source_weight, target_weight, source_bounds, target_bounds, kept_pairs):
    src_tile, tgt_tile, occupied = tile_layout(source_bounds, target_bounds, kept_pairs)
    src_count = N_ROW * TS
    tgt_count = N_COL * TT
    inv_root = 1.0 / math.sqrt(D)
    x_tiles = source_emb.reshape(src_count, TILE, D)[src_tile].astype(jnp.float32)
    y_tiles = target_emb.reshape(tgt_count, TILE, D)[tgt_tile].astype(jnp.float32)
    tile_cost = -inv_root * jnp.einsum('kid,kjd->kij', x_tiles, y_tiles)
    is_live = occupied[:, None, None]

    def rows_of(vector):
        return vector.reshape(src_count, TILE)[src_tile]

    def columns_of(vector):
        return vector.reshape(tgt_count, TILE)[tgt_tile]

    def source_step(target_pot):
        scores = jnp.where(is_live, (columns_of(target_pot)[:, None, :] - tile_cost) / temper, sentinel)
        largest = jax.ops.segment_max(lax.optimization_barrier(jnp.max(scores, axis=2)), src_tile, num_segments=src_count)
        shifted = jnp.where(is_live, jnp.exp(scores - largest[src_tile][:, :, None]), 0.0)
        totals = jax.ops.segment_sum(lax.optimization_barrier(jnp.sum(shifted, axis=2)), src_tile, num_segments=src_count)
        return (-temper * (largest + jnp.log(totals))).reshape(-1)

    def target_step(source_pot):
        scores = jnp.where(is_live, (rows_of(source_pot)[:, :, None] - tile_cost) / temper, sentinel)
        largest = jax.ops.segment_max(lax.optimization_barrier(jnp.max(scores, axis=1)), tgt_tile, num_segments=tgt_count)
        shifted = jnp.where(is_live, jnp.exp(scores - largest[tgt_tile][:, None, :]), 0.0)
        totals = jax.ops.segment_sum(lax.optimization_barrier(jnp.sum(shifted, axis=1)), tgt_tile, num_segments=tgt_count)
        return (-temper * (largest + jnp.log(totals))).reshape(-1)

    def transport(row_pot, column_pot):
        return jnp.where(is_live, jnp.exp((row_pot[:, :, None] + column_pot[:, None, :] - tile_cost) / temper), 0.0)
    first_source = source_step(warm_start)
    first_target = target_step(first_source)
    second_source = source_step(first_target)
    second_target = target_step(second_source)
    bar_cost = transport(rows_of(second_source), columns_of(second_target)) * columns_of(target_weight)[:, None, :]
    adjoint_late = source_weight - jax.ops.segment_sum(lax.optimization_barrier(jnp.sum(bar_cost, axis=2)), src_tile, num_segments=src_count).reshape(-1)
    addend = transport(rows_of(second_source), columns_of(first_target)) * rows_of(adjoint_late)[:, :, None]
    adjoint_mid = -jax.ops.segment_sum(lax.optimization_barrier(jnp.sum(addend, axis=1)), tgt_tile, num_segments=tgt_count).reshape(-1)
    bar_cost = bar_cost + addend
    addend = transport(rows_of(first_source), columns_of(first_target)) * columns_of(adjoint_mid)[:, None, :]
    adjoint_early = -jax.ops.segment_sum(lax.optimization_barrier(jnp.sum(addend, axis=2)), src_tile, num_segments=src_count).reshape(-1)
    bar_cost = bar_cost + addend
    bar_cost = bar_cost + transport(rows_of(first_source), columns_of(warm_start)) * rows_of(adjoint_early)[:, :, None]
    rounded = lax.optimization_barrier(bar_cost.astype(jnp.bfloat16)).astype(jnp.float32)
    source_part = -inv_root * jnp.einsum('kij,kjd->kid', rounded, y_tiles)
    target_part = -inv_root * jnp.einsum('kij,kid->kjd', rounded, x_tiles)
    grad_source = jax.ops.segment_sum(source_part, src_tile, num_segments=src_count).reshape(NS, D)
    grad_target = jax.ops.segment_sum(target_part, tgt_tile, num_segments=tgt_count).reshape(NT, D)
    return (grad_source.astype(jnp.bfloat16), grad_target.astype(jnp.bfloat16))
```

```python
import functools
import math

import jax
import jax.numpy as jnp
from jax import lax
from jax.experimental import pallas as pl
from jax.experimental.pallas import tpu as pltpu
from jax.sharding import PartitionSpec as P

TILE = 512
HALF = 256
BLOCK = 4
LANES = 128
ROWS = 64
LIMIT = 24 * 1024 * 1024
LOWEST = -1e30
F32 = jnp.float32
NT_DIMS = (((1,), (1,)), ((), ()))
NN_DIMS = (((1,), (0,)), ((), ()))
TN_DIMS = (((0,), (0,)), ((), ()))


def kept_range(first_cut, second_cut, straight, tile):
    is_low = (tile < first_cut).astype(jnp.int32) == straight
    return jnp.where(is_low, 0, second_cut), jnp.where(is_low, second_cut, BLOCK)


def read_meta(meta_ref):
    return meta_ref[0, 0], meta_ref[0, 1], meta_ref[0, 2]


def to_column(row):
    return jnp.broadcast_to(row, (LANES, row.shape[1])).T


def lane_sums(values):
    return jnp.sum(values.T, axis=0, keepdims=True)


def total(refs, index):
    value = refs[0][index]
    for ref in refs[1:]:
        value = value + ref[index]
    return value


def weighted_rows(e_ref, meta, vector_ref, out_ref):
    for s in range(BLOCK):
        low, high = kept_range(*meta, s)
        for start in range(0, TILE, HALF):

            def step(t, acc):
                vector = vector_ref[t]
                parts = []
                for at in range(0, HALF, ROWS):
                    e = e_ref[s, t, start + at : start + at + ROWS, :]
                    parts.append(
                        acc[at : at + ROWS]
                        + (e[:, :LANES] * vector[:, :LANES] + e[:, LANES:] * vector[:, LANES:])
                    )
                return jnp.concatenate(parts, axis=0)

            acc = lax.fori_loop(low, high, step, jnp.zeros((HALF, LANES), F32))
            out_ref[s, :, start : start + HALF] = lane_sums(acc)


def weighted_columns(e_ref, meta, rows, column_ref, eight_ref):
    eight_ref[...] = jnp.zeros_like(eight_ref)
    for s in range(BLOCK):
        low, high = kept_range(*meta, s)
        column_ref[...] = to_column(rows(s))

        def step(t, carry):
            left = jnp.zeros((8, LANES), F32)
            right = jnp.zeros((8, LANES), F32)
            for at in range(0, TILE, ROWS):
                e = e_ref[s, t, at : at + ROWS, :]
                u = column_ref[at : at + ROWS, :]
                left = left + jnp.sum((e[:, :LANES] * u).reshape(-1, 8, LANES), axis=0)
                right = right + jnp.sum((e[:, LANES:] * u).reshape(-1, 8, LANES), axis=0)
            eight_ref[t, :, :LANES] += left
            eight_ref[t, :, LANES:] += right
            return carry

        lax.fori_loop(low, high, step, 0)


def first_source_kernel(
    x_ref, y_ref, warm_ref, sb_ref, tb_ref, kp_ref, e_ref, out_ref, meta_ref, largest_ref
):
    row_pos = lax.axis_index("row")
    col_pos = lax.axis_index("col")
    rep_pos = lax.axis_index("rep")
    first_cut = sb_ref[2 * row_pos + 1] - BLOCK * row_pos
    second_cut = tb_ref[2 * col_pos + 1] - BLOCK * col_pos

    def look(i, found):
        here = (kp_ref[i, 0] == 2 * row_pos) & (kp_ref[i, 1] == 2 * col_pos)
        return found | here.astype(jnp.int32)

    straight = lax.fori_loop(0, kp_ref.shape[0], look, jnp.int32(0))
    lanes = lax.broadcasted_iota(jnp.int32, meta_ref.shape, 1)
    meta_ref[...] = jnp.where(lanes == 0, first_cut, jnp.where(lanes == 1, second_cut, straight))
    meta = (first_cut, second_cut, straight)
    inv_root = x_ref.shape[1] ** (-0.5)
    for s in range(BLOCK):
        low, high = kept_range(*meta, s)
        largest_ref[...] = jnp.full_like(largest_ref, LOWEST)

        def score(t, carry):
            warm = warm_ref[2 * t + rep_pos]
            y = y_ref[pl.ds(pl.multiple_of(t * TILE + rep_pos * HALF, HALF), HALF), :]
            for at in range(0, TILE, HALF):
                x = x_ref[s * TILE + at : s * TILE + at + HALF, :]
                scores = lax.dot_general(x, y, NT_DIMS, preferred_element_type=F32) * inv_root
                e_ref[s, t, at : at + HALF, :] = scores
                shifted = scores + warm
                largest_ref[at : at + HALF, :] = jnp.maximum(
                    largest_ref[at : at + HALF, :],
                    jnp.maximum(shifted[:, :LANES], shifted[:, LANES:]),
                )
            return carry

        lax.fori_loop(low, high, score, 0)
        for start in range(0, TILE, HALF):
            largest = jnp.max(largest_ref[start : start + HALF, :], axis=1, keepdims=True)
            largest = jnp.broadcast_to(largest, (HALF, LANES))

            def step(t, acc):
                warm = warm_ref[2 * t + rep_pos]
                parts = []
                for at in range(0, HALF, ROWS):
                    e = e_ref[s, t, start + at : start + at + ROWS, :]
                    m = largest[at : at + ROWS]
                    parts.append(
                        acc[at : at + ROWS]
                        + jnp.exp(e[:, :LANES] + warm[:, :LANES] - m)
                        + jnp.exp(e[:, LANES:] + warm[:, LANES:] - m)
                    )
                return jnp.concatenate(parts, axis=0)

            acc = lax.fori_loop(low, high, step, jnp.zeros((HALF, LANES), F32))
            out_ref[s, :, start : start + HALF] = largest.T[:1]
            out_ref[BLOCK + s, :, start : start + HALF] = lane_sums(acc)


def combine(refs, at, offset):
    largest = refs[0][at]
    for ref in refs[1:]:
        largest = jnp.maximum(largest, ref[at])
    sums = refs[0][offset + at] * jnp.exp(refs[0][at] - largest)
    for ref in refs[1:]:
        sums = sums + ref[offset + at] * jnp.exp(ref[at] - largest)
    return -(largest + jnp.log(sums))


def first_target_kernel(count, *args):
    parts = args[:count]
    score_ref, meta_ref, e_ref, out_ref, column_ref, eight_ref = args[count:]
    meta = read_meta(meta_ref)
    eight_ref[...] = jnp.full_like(eight_ref, LOWEST)
    for s in range(BLOCK):
        low, high = kept_range(*meta, s)
        column_ref[s] = to_column(combine(parts, s, BLOCK))

        def peak(t, carry):
            left = eight_ref[t, :, :LANES]
            right = eight_ref[t, :, LANES:]
            for at in range(0, TILE, ROWS):
                e = score_ref[s, t, at : at + ROWS, :]
                u = column_ref[s, at : at + ROWS, :]
                left = jnp.maximum(left, jnp.max((e[:, :LANES] + u).reshape(-1, 8, LANES), axis=0))
                right = jnp.maximum(
                    right, jnp.max((e[:, LANES:] + u).reshape(-1, 8, LANES), axis=0)
                )
            eight_ref[t, :, :LANES] = left
            eight_ref[t, :, LANES:] = right
            return carry

        lax.fori_loop(low, high, peak, 0)
    for t in range(BLOCK):
        out_ref[t] = jnp.max(eight_ref[t], axis=0, keepdims=True)
    eight_ref[...] = jnp.zeros_like(eight_ref)
    for s in range(BLOCK):
        low, high = kept_range(*meta, s)

        def step(t, carry):
            largest = out_ref[t]
            left = jnp.zeros((8, LANES), F32)
            right = jnp.zeros((8, LANES), F32)
            for at in range(0, TILE, ROWS):
                e = score_ref[s, t, at : at + ROWS, :]
                u = column_ref[s, at : at + ROWS, :]
                e_left = jnp.exp(e[:, :LANES] + u - largest[:, :LANES])
                e_right = jnp.exp(e[:, LANES:] + u - largest[:, LANES:])
                e_ref[s, t, at : at + ROWS, :LANES] = e_left
                e_ref[s, t, at : at + ROWS, LANES:] = e_right
                left = left + jnp.sum(e_left.reshape(-1, 8, LANES), axis=0)
                right = right + jnp.sum(e_right.reshape(-1, 8, LANES), axis=0)
            eight_ref[t, :, :LANES] += left
            eight_ref[t, :, LANES:] += right
            return carry

        lax.fori_loop(low, high, step, 0)
    for t in range(BLOCK):
        out_ref[BLOCK + t] = jnp.sum(eight_ref[t], axis=0, keepdims=True)


def second_source_kernel(count, *args):
    parts = args[:count]
    warm_ref, e_ref, meta_ref, out_ref, q_ref, wq_ref = args[count:]
    rep_pos = lax.axis_index("rep")
    for t in range(BLOCK):
        potential = combine(parts, t, BLOCK)
        q = jnp.exp(parts[0][t] + potential)
        q_ref[t] = q
        wq_ref[t] = q * jnp.exp(warm_ref[2 * t + rep_pos] - potential)
    weighted_rows(e_ref, read_meta(meta_ref), q_ref, out_ref)


def second_target_kernel(count, *args):
    parts = args[:count]
    e_ref, meta_ref, q_ref, out_ref, a_ref, column_ref, eight_ref = args[count:]
    for s in range(BLOCK):
        a_ref[s] = 1.0 / total(parts, s)
    weighted_columns(e_ref, read_meta(meta_ref), lambda s: a_ref[s], column_ref, eight_ref)
    for t in range(BLOCK):
        out_ref[t] = q_ref[t] * jnp.sum(eight_ref[t], axis=0, keepdims=True)


def late_kernel(count, *args):
    parts = args[:count]
    e_ref, meta_ref, q_ref, weight_ref, out_ref, p_ref = args[count:]
    rep_pos = lax.axis_index("rep")
    for t in range(BLOCK):
        p_ref[t] = weight_ref[2 * t + rep_pos] * q_ref[t] / total(parts, t)
    weighted_rows(e_ref, read_meta(meta_ref), p_ref, out_ref)


def mid_kernel(count, *args):
    parts = args[:count]
    e_ref, meta_ref, q_ref, a_ref, weight_ref, out_ref, b_ref, column_ref, eight_ref = args[count:]
    for s in range(BLOCK):
        a = a_ref[s]
        b_ref[s] = a * (weight_ref[s] - a * total(parts, s))
    weighted_columns(e_ref, read_meta(meta_ref), lambda s: b_ref[s], column_ref, eight_ref)
    for t in range(BLOCK):
        out_ref[t] = -q_ref[t] * jnp.sum(eight_ref[t], axis=0, keepdims=True)


def early_kernel(count, *args):
    parts = args[:count]
    e_ref, meta_ref, q_ref, out_ref, h_ref = args[count:]
    for t in range(BLOCK):
        h_ref[t] = q_ref[t] * total(parts, t)
    weighted_rows(e_ref, read_meta(meta_ref), h_ref, out_ref)


def gradient_kernel(count, others, rows, *args):
    parts = args[:count]
    args = args[count:]
    x_ref, y_ref, e_ref, meta_ref, a_ref, b_ref, p_ref, q_ref, h_ref, wq_ref = args[:10]
    source_refs = args[10 : 10 + others]
    target_refs = args[10 + others : 10 + others + rows]
    a_col, b_col, early_col, bar_ref, source_acc, target_acc = args[10 + others + rows :]
    rep_pos = lax.axis_index("rep")
    own = lax.axis_index("col") * 2 + rep_pos
    row_pos = lax.axis_index("row")
    meta = read_meta(meta_ref)
    inv_root = x_ref.shape[1] ** (-0.5)
    target_acc[...] = jnp.zeros_like(target_acc)
    source_acc[...] = jnp.zeros_like(source_acc)
    for s in range(BLOCK):
        low, high = kept_range(*meta, s)
        a_col[...] = to_column(a_ref[s])
        b_col[...] = to_column(b_ref[s])
        early_col[...] = to_column(-total(parts, s))

        def step(t, carry):
            p, q, h, wq = p_ref[t], q_ref[t], h_ref[t], wq_ref[t]
            for at in range(0, TILE, ROWS):
                e = e_ref[s, t, at : at + ROWS, :]
                a = a_col[at : at + ROWS, :]
                b = b_col[at : at + ROWS, :]
                early = early_col[at : at + ROWS, :]
                for side in (slice(0, LANES), slice(LANES, HALF)):
                    factor = a * p[:, side] + b * q[:, side] + (h[:, side] + early * wq[:, side])
                    bar_ref[at : at + ROWS, side] = (e[:, side] * factor).astype(jnp.bfloat16)
            y = y_ref[pl.ds(pl.multiple_of(t * TILE + rep_pos * HALF, HALF), HALF), :]
            bar = bar_ref[...]
            source_acc[s * TILE : (s + 1) * TILE, :] += lax.dot_general(
                bar, y, NN_DIMS, preferred_element_type=F32
            )
            x = x_ref[s * TILE : (s + 1) * TILE, :]
            begin = pl.multiple_of(t * HALF, HALF)
            target_acc[pl.ds(begin, HALF), :] += lax.dot_general(
                bar, x, TN_DIMS, preferred_element_type=F32
            )
            return carry

        lax.fori_loop(low, high, step, 0)
    for refs, acc, position in (
        (source_refs, source_acc, own),
        (target_refs, target_acc, row_pos),
    ):
        piece = acc.shape[0] // len(refs)
        for k, ref in enumerate(refs):
            begin = pl.multiple_of((position ^ k) * piece, piece)
            ref[...] = (-inv_root * acc[pl.ds(begin, piece), :]).astype(ref.dtype)


def place_kernel(rows, *args):
    own, other, out_ref = args[:rows], args[rows : 2 * rows], args[2 * rows]
    rep_pos = lax.axis_index("rep")
    row_pos = lax.axis_index("row")
    piece = own[0].shape[0]
    per_tile = HALF // piece
    for refs, rep in ((own, rep_pos), (other, 1 - rep_pos)):
        for k, ref in enumerate(refs):
            at = row_pos ^ k
            begin = (at // per_tile) * TILE + rep * HALF + (at % per_tile) * piece
            out_ref[pl.ds(pl.multiple_of(begin, piece), piece), :] = ref[...]


def in_vmem(value):
    return pltpu.with_memory_space_constraint(value, pltpu.VMEM)


def call(kernel, name, outs, scratch, args, spaces=None):
    specs = [
        pl.BlockSpec(memory_space=pltpu.VMEM if spaces is None else spaces[i])
        for i in range(len(args))
    ]
    args = [
        in_vmem(value) if spaces is None or spaces[i] == pltpu.VMEM else value
        for i, value in enumerate(args)
    ]
    return pl.pallas_call(
        kernel,
        name=name,
        out_shape=[pltpu.VMEM(shape, dtype) for shape, dtype in outs],
        in_specs=specs,
        out_specs=[pl.BlockSpec(memory_space=pltpu.VMEM) for _ in outs],
        scratch_shapes=scratch,
        compiler_params=pltpu.CompilerParams(vmem_limit_bytes=LIMIT),
    )(*args)


def shards(
    sizes,
    source_emb,
    target_emb,
    warm_start,
    source_weight,
    target_weight,
    source_bounds,
    target_bounds,
    kept_pairs,
):
    width = source_emb.shape[1]

    def swap(value, axes, k):
        count = math.prod(sizes[axis] for axis in axes)
        return lax.ppermute(value, axes, [(i, i ^ k) for i in range(count)])

    def spread(value, axes):
        count = math.prod(sizes[axis] for axis in axes)
        return [value] + [swap(value, axes, k) for k in range(1, count)]

    over_source = ("col", "rep")
    over_target = ("row",)
    warm = warm_start.reshape(2 * BLOCK, 1, HALF)
    target_weight = target_weight.reshape(2 * BLOCK, 1, HALF)
    source_weight = source_weight.reshape(BLOCK, 1, TILE)
    source_vector = ((BLOCK, 1, TILE), F32)
    target_vector = ((BLOCK, 1, HALF), F32)
    matrix = ((BLOCK, BLOCK, TILE, HALF), F32)
    column = pltpu.VMEM((TILE, LANES), F32)
    eight = pltpu.VMEM((BLOCK, 8, HALF), F32)
    vmem, smem = pltpu.VMEM, pltpu.SMEM

    score, packed, meta = call(
        first_source_kernel,
        "first_source",
        [matrix, ((2 * BLOCK, 1, TILE), F32), ((8, LANES), jnp.int32)],
        [column],
        [source_emb, target_emb, warm, source_bounds, target_bounds, kept_pairs],
        [vmem, vmem, vmem, smem, smem, smem],
    )
    parts = spread(packed, over_source)
    n_source = len(parts)
    e, packed = call(
        functools.partial(first_target_kernel, n_source),
        "first_target",
        [matrix, ((2 * BLOCK, 1, HALF), F32)],
        [pltpu.VMEM((BLOCK, TILE, LANES), F32), eight],
        [*parts, score, meta],
    )
    parts = spread(packed, over_target)
    n_target = len(parts)
    sums, q, wq = call(
        functools.partial(second_source_kernel, n_target),
        "second_source",
        [source_vector, target_vector, target_vector],
        [],
        [*parts, warm, e, meta],
    )
    parts = spread(sums, over_source)
    sums, a = call(
        functools.partial(second_target_kernel, n_source),
        "second_target",
        [target_vector, source_vector],
        [column, eight],
        [*parts, e, meta, q],
    )
    parts = spread(sums, over_target)
    sums, p = call(
        functools.partial(late_kernel, n_target),
        "late",
        [source_vector, target_vector],
        [],
        [*parts, e, meta, q, target_weight],
    )
    parts = spread(sums, over_source)
    sums, b = call(
        functools.partial(mid_kernel, n_source),
        "mid",
        [target_vector, source_vector],
        [column, eight],
        [*parts, e, meta, q, a, source_weight],
    )
    parts = spread(sums, over_target)
    sums, h = call(
        functools.partial(early_kernel, n_target),
        "early",
        [source_vector, target_vector],
        [],
        [*parts, e, meta, q],
    )
    parts = spread(sums, over_source)
    rows = sizes["row"]
    source_piece = BLOCK * TILE // n_source
    target_piece = BLOCK * HALF // rows
    outs = call(
        functools.partial(gradient_kernel, n_source, n_source, rows),
        "gradient",
        [((source_piece, width), F32 if k == 0 else jnp.bfloat16) for k in range(n_source)]
        + [((target_piece, width), F32 if k == 0 else jnp.bfloat16) for k in range(rows)],
        [
            column,
            column,
            column,
            pltpu.VMEM((TILE, HALF), jnp.bfloat16),
            pltpu.VMEM((BLOCK * TILE, width), F32),
            pltpu.VMEM((BLOCK * HALF, width), F32),
        ],
        [*parts, source_emb, target_emb, e, meta, a, b, p, q, h, wq],
    )
    source_parts, target_parts = outs[:n_source], outs[n_source:]

    def reduced(pieces, axes):
        value = pieces[0]
        for k in range(1, len(pieces)):
            value = value + swap(pieces[k], axes, k).astype(F32)
        return value.astype(jnp.bfloat16)

    target_rows = reduced(target_parts, over_target)
    grad_source = reduced(source_parts, over_source)
    pieces = spread(target_rows, over_target)
    pieces = pieces + [swap(value, ("rep",), 1) for value in pieces]
    grad_target = pl.pallas_call(
        functools.partial(place_kernel, rows),
        name="place",
        out_shape=jax.ShapeDtypeStruct(target_emb.shape, jnp.bfloat16),
        in_specs=[pl.BlockSpec(memory_space=pltpu.VMEM)] * len(pieces),
        out_specs=pl.BlockSpec(memory_space=pltpu.VMEM),
        compiler_params=pltpu.CompilerParams(vmem_limit_bytes=LIMIT),
    )(*pieces)
    return grad_source, grad_target


def solution(mesh):
    return jax.shard_map(
        functools.partial(shards, dict(mesh.shape)),
        mesh=mesh,
        in_specs=(
            P(("groups", "row"), None),
            P(("groups", "col"), None),
            P(("groups", "col")),
            P(("groups", "row")),
            P(("groups", "col")),
            P("groups"),
            P("groups"),
            P("groups", None),
        ),
        out_specs=(P(("groups", "row", "col", "rep"), None), P(("groups", "col"), None)),
        check_vma=False,
    )
```

```python
import functools
import math

import jax
import jax.numpy as jnp
from jax import lax
from jax.experimental import pallas as pl
from jax.experimental.pallas import tpu as pltpu
from jax.sharding import PartitionSpec as P

TILE = 512
HALF = 256
BLOCK = 4
LANES = 128
ROWS = 64
LIMIT = 24 * 1024 * 1024
LOWEST = -1e30
F32 = jnp.float32
NT_DIMS = (((1,), (1,)), ((), ()))
NN_DIMS = (((1,), (0,)), ((), ()))
TN_DIMS = (((0,), (0,)), ((), ()))


def kept_targets(meta, s):
    first_cut, second_cut, straight = meta
    is_low = (s < first_cut).astype(jnp.int32) == straight
    return jnp.where(is_low, 0, second_cut), jnp.where(is_low, second_cut, BLOCK)


def kept_sources(meta, t):
    first_cut, second_cut, straight = meta
    is_low = (t < second_cut).astype(jnp.int32) == straight
    return jnp.where(is_low, 0, first_cut), jnp.where(is_low, first_cut, BLOCK)


def tile_lanes(t):
    return pl.ds(pl.multiple_of(t * HALF, HALF), HALF)


def read_meta(meta_ref):
    return meta_ref[0, 0], meta_ref[0, 1], meta_ref[0, 2]


def to_column(row):
    return jnp.broadcast_to(row, (LANES, row.shape[1])).T


def lane_sums(values):
    return jnp.sum(values.T, axis=0, keepdims=True)


def total(refs, index):
    value = refs[0][index]
    for ref in refs[1:]:
        value = value + ref[index]
    return value


def for_widths(low, high, body):
    for n in range(1, BLOCK):
        pl.when(high - low == n)(functools.partial(body, n))


def weighted_rows(e_ref, meta, vector_ref, out_ref):
    def one(s, carry):
        low, high = kept_targets(meta, s)

        def body(n):
            vectors = [vector_ref[low + i] for i in range(n)]
            for at in range(0, TILE, LANES):
                acc = None
                for i in range(n):
                    e = e_ref[s, at : at + LANES, tile_lanes(low + i)]
                    term = e[:, :LANES] * vectors[i][:, :LANES] + e[:, LANES:] * vectors[i][:, LANES:]
                    acc = term if acc is None else acc + term
                out_ref[s, :, at : at + LANES] = lane_sums(acc)

        for_widths(low, high, body)
        return carry

    lax.fori_loop(0, BLOCK, one, 0)


def eight_rows(values, reduce):
    return reduce(values.reshape(-1, 8, LANES), axis=0)


def weighted_columns(e_ref, meta, column_ref, scale_ref, out_ref):
    def one(t, carry):
        low, high = kept_sources(meta, t)

        def step(s, acc):
            left, right = acc
            for at in range(0, TILE, ROWS):
                e = e_ref[s, at : at + ROWS, tile_lanes(t)]
                u = column_ref[s, at : at + ROWS, :]
                left = left + eight_rows(e[:, :LANES] * u, jnp.sum)
                right = right + eight_rows(e[:, LANES:] * u, jnp.sum)
            return left, right

        zero = jnp.zeros((8, LANES), F32)
        left, right = lax.fori_loop(low, high, step, (zero, zero))
        scale = scale_ref[t]
        out_ref[t, :, :LANES] = scale[:, :LANES] * jnp.sum(left, axis=0, keepdims=True)
        out_ref[t, :, LANES:] = scale[:, LANES:] * jnp.sum(right, axis=0, keepdims=True)
        return carry

    lax.fori_loop(0, BLOCK, one, 0)


def first_source_kernel(
    x_hbm,
    y_hbm,
    warm_hbm,
    sb_hbm,
    tb_hbm,
    kp_hbm,
    score_ref,
    out_ref,
    meta_ref,
    x_ref,
    y_ref,
    warm_ref,
    sb_ref,
    tb_ref,
    kp_ref,
    x_sems,
    y_sems,
    warm_sems,
    bound_sems,
):
    row_pos = lax.axis_index("row")
    col_pos = lax.axis_index("col")
    rep_pos = lax.axis_index("rep")
    bounds = [
        pltpu.make_async_copy(source, target, bound_sems.at[i])
        for i, (source, target) in enumerate(
            ((sb_hbm, sb_ref), (tb_hbm, tb_ref), (kp_hbm, kp_ref))
        )
    ]
    x_copies, y_copies, warm_copies = [], [], []
    for t in range(BLOCK):
        begin = pl.multiple_of(t * TILE + rep_pos * HALF, HALF)
        y_copies.append(
            pltpu.make_async_copy(
                y_hbm.at[pl.ds(begin, HALF)], y_ref.at[pl.ds(t * HALF, HALF)], y_sems.at[t]
            )
        )
        warm_copies.append(
            pltpu.make_async_copy(warm_hbm.at[2 * t + rep_pos], warm_ref.at[t], warm_sems.at[t])
        )
        x_copies.append(
            pltpu.make_async_copy(
                x_hbm.at[pl.ds(t * TILE, TILE)], x_ref.at[pl.ds(t * TILE, TILE)], x_sems.at[t]
            )
        )
    for copy in bounds + y_copies + x_copies[:1] + warm_copies + x_copies[1:]:
        copy.start()
    for copy in bounds:
        copy.wait()
    first_cut = sb_ref[2 * row_pos + 1] - BLOCK * row_pos
    second_cut = tb_ref[2 * col_pos + 1] - BLOCK * col_pos

    def look(i, found):
        here = (kp_ref[0, i] == 2 * row_pos) & (kp_ref[1, i] == 2 * col_pos)
        return found | here.astype(jnp.int32)

    straight = lax.fori_loop(0, kp_ref.shape[1], look, jnp.int32(0))
    lanes = lax.broadcasted_iota(jnp.int32, meta_ref.shape, 1)
    meta_ref[...] = jnp.where(lanes == 0, first_cut, jnp.where(lanes == 1, second_cut, straight))
    meta = (first_cut, second_cut, straight)
    inv_root = x_ref.shape[1] ** (-0.5)
    for copy in y_copies:
        copy.wait()
    for s in range(BLOCK):
        x_copies[s].wait()
        score_ref[s] = inv_root * lax.dot_general(
            x_ref[s * TILE : (s + 1) * TILE, :],
            y_ref[...],
            NT_DIMS,
            preferred_element_type=F32,
        )
    for copy in warm_copies:
        copy.wait()

    def one(s, carry):
        low, high = kept_targets(meta, s)

        def body(n):
            warm = [warm_ref[low + i] for i in range(n)]
            for at in range(0, TILE, LANES):
                largest = None
                for i in range(n):
                    e = score_ref[s, at : at + LANES, tile_lanes(low + i)]
                    term = jnp.maximum(
                        e[:, :LANES] + warm[i][:, :LANES], e[:, LANES:] + warm[i][:, LANES:]
                    )
                    largest = term if largest is None else jnp.maximum(largest, term)
                largest = jnp.max(largest, axis=1, keepdims=True)
                largest = jnp.broadcast_to(largest, (LANES, LANES))
                acc = None
                for i in range(n):
                    e = score_ref[s, at : at + LANES, tile_lanes(low + i)]
                    term = jnp.exp(e[:, :LANES] + warm[i][:, :LANES] - largest) + jnp.exp(
                        e[:, LANES:] + warm[i][:, LANES:] - largest
                    )
                    acc = term if acc is None else acc + term
                out_ref[s, :, at : at + LANES] = largest.T[:1]
                out_ref[BLOCK + s, :, at : at + LANES] = lane_sums(acc)

        for_widths(low, high, body)
        return carry

    lax.fori_loop(0, BLOCK, one, 0)


def combine(refs, at, offset):
    largest = refs[0][at]
    for ref in refs[1:]:
        largest = jnp.maximum(largest, ref[at])
    sums = refs[0][offset + at] * jnp.exp(refs[0][at] - largest)
    for ref in refs[1:]:
        sums = sums + ref[offset + at] * jnp.exp(ref[at] - largest)
    return -(largest + jnp.log(sums))


def first_target_kernel(count, *args):
    parts = args[:count]
    score_ref, meta_ref, e_ref, out_ref, column_ref = args[count:]
    meta = read_meta(meta_ref)
    for s in range(BLOCK):
        column_ref[s] = to_column(combine(parts, s, BLOCK))

    def one(t, carry):
        low, high = kept_sources(meta, t)

        def peak(s, acc):
            left, right = acc
            for at in range(0, TILE, ROWS):
                e = score_ref[s, at : at + ROWS, tile_lanes(t)]
                u = column_ref[s, at : at + ROWS, :]
                left = jnp.maximum(left, eight_rows(e[:, :LANES] + u, jnp.max))
                right = jnp.maximum(right, eight_rows(e[:, LANES:] + u, jnp.max))
            return left, right

        lowest = jnp.full((8, LANES), LOWEST, F32)
        left, right = lax.fori_loop(low, high, peak, (lowest, lowest))
        left = jnp.max(left, axis=0, keepdims=True)
        right = jnp.max(right, axis=0, keepdims=True)
        out_ref[t, :, :LANES] = left
        out_ref[t, :, LANES:] = right

        def step(s, acc):
            left_sum, right_sum = acc
            for at in range(0, TILE, ROWS):
                e = score_ref[s, at : at + ROWS, tile_lanes(t)]
                u = column_ref[s, at : at + ROWS, :]
                e_left = jnp.exp(e[:, :LANES] + u - left)
                e_right = jnp.exp(e[:, LANES:] + u - right)
                e_ref[s, at : at + ROWS, tile_lanes(t)] = jnp.concatenate([e_left, e_right], axis=1)
                left_sum = left_sum + eight_rows(e_left, jnp.sum)
                right_sum = right_sum + eight_rows(e_right, jnp.sum)
            return left_sum, right_sum

        zero = jnp.zeros((8, LANES), F32)
        left_sum, right_sum = lax.fori_loop(low, high, step, (zero, zero))
        out_ref[BLOCK + t, :, :LANES] = jnp.sum(left_sum, axis=0, keepdims=True)
        out_ref[BLOCK + t, :, LANES:] = jnp.sum(right_sum, axis=0, keepdims=True)
        return carry

    lax.fori_loop(0, BLOCK, one, 0)


def second_source_kernel(count, *args):
    parts = args[:count]
    warm_ref, e_ref, meta_ref, out_ref, q_ref, wq_ref = args[count:]
    for t in range(BLOCK):
        potential = combine(parts, t, BLOCK)
        q = jnp.exp(parts[0][t] + potential)
        q_ref[t] = q
        wq_ref[t] = q * jnp.exp(warm_ref[t] - potential)
    weighted_rows(e_ref, read_meta(meta_ref), q_ref, out_ref)


def second_target_kernel(count, *args):
    parts = args[:count]
    e_ref, meta_ref, q_ref, out_ref, a_ref, column_ref = args[count:]
    for s in range(BLOCK):
        a = 1.0 / total(parts, s)
        a_ref[s] = a
        column_ref[s] = to_column(a)
    weighted_columns(e_ref, read_meta(meta_ref), column_ref, q_ref, out_ref)


def late_kernel(count, *args):
    parts = args[:count]
    e_ref, meta_ref, q_ref, weight_ref, out_ref, p_ref = args[count:]
    rep_pos = lax.axis_index("rep")
    for t in range(BLOCK):
        p_ref[t] = weight_ref[2 * t + rep_pos] * q_ref[t] / total(parts, t)
    weighted_rows(e_ref, read_meta(meta_ref), p_ref, out_ref)


def mid_kernel(count, *args):
    parts = args[:count]
    e_ref, meta_ref, q_ref, a_ref, weight_ref, out_ref, column_ref = args[count:]
    for s in range(BLOCK):
        a = a_ref[s]
        column_ref[s] = to_column(a * (weight_ref[s] - a * total(parts, s)))
    weighted_columns(e_ref, read_meta(meta_ref), column_ref, q_ref, out_ref)


def early_kernel(count, *args):
    parts = args[:count]
    e_ref, meta_ref, q_ref, out_ref, h_ref = args[count:]
    for t in range(BLOCK):
        h_ref[t] = -q_ref[t] * total(parts, t)
    weighted_rows(e_ref, read_meta(meta_ref), h_ref, out_ref)


def target_gradient_kernel(part, count, *args):
    if count:
        parts = args[:count]
        x_ref, e_ref, meta_ref, a_ref, b_ref, p_ref, q_ref, h_ref, wq_ref = args[count : count + 9]
        bar_ref, early_ref, *out_refs = args[count + 9 :]
        for s in range(BLOCK):
            early_ref[s] = to_column(-total(parts, s))
    else:
        x_ref, e_ref, meta_ref, a_ref, b_ref, p_ref, q_ref, h_ref, wq_ref = args[:9]
        early_ref, _, bar_ref, *out_refs = args[9:]
    row_pos = lax.axis_index("row")
    per_tile = len(out_refs)
    t = (row_pos // per_tile) ^ part
    low, high = kept_sources(read_meta(meta_ref), t)
    p, q, h, wq = p_ref[t], q_ref[t], h_ref[t], wq_ref[t]
    for s in range(BLOCK):

        @pl.when((s >= low) & (s < high))
        def _():
            for at in range(0, TILE, ROWS):
                e = e_ref[s, at : at + ROWS, tile_lanes(t)]
                a = a_ref[s, at : at + ROWS, :]
                b = b_ref[s, at : at + ROWS, :]
                early = early_ref[s, at : at + ROWS, :]
                sides = []
                for side in (slice(0, LANES), slice(LANES, HALF)):
                    factor = a * p[:, side] + b * q[:, side] + (h[:, side] + early * wq[:, side])
                    sides.append((e[:, side] * factor).astype(jnp.bfloat16))
                bar_ref[s, at : at + ROWS, tile_lanes(t)] = jnp.concatenate(sides, axis=1)

        @pl.when((s < low) | (s >= high))
        def _():
            bar_ref[s, :, tile_lanes(t)] = jnp.zeros((TILE, HALF), jnp.bfloat16)

    bar = bar_ref[:, :, tile_lanes(t)].reshape(BLOCK * TILE, HALF)
    inv_root = x_ref.shape[1] ** (-0.5)
    result = -inv_root * lax.dot_general(bar, x_ref[...], TN_DIMS, preferred_element_type=F32)
    if per_tile == 1:
        out_refs[0][...] = result.astype(out_refs[0].dtype)
        return
    piece = HALF // per_tile
    for i, ref in enumerate(out_refs):
        at = (row_pos % per_tile) ^ i
        for j in range(per_tile):

            @pl.when(at == j)
            def _():
                ref[...] = result[j * piece : (j + 1) * piece, :].astype(ref.dtype)


def source_gradient_kernel(bar_ref, y_ref, near_ref, far_ref, acc_ref):
    inv_root = y_ref.shape[1] ** (-0.5)
    col_pos = lax.axis_index("col")
    rep_pos = lax.axis_index("rep")
    for s in range(BLOCK):
        acc_ref[s * TILE : (s + 1) * TILE, :] = -inv_root * lax.dot_general(
            bar_ref[s], y_ref[...], NN_DIMS, preferred_element_type=F32
        )
    piece = near_ref.shape[1]
    for d in range(near_ref.shape[0]):
        at = 2 * (col_pos ^ d)
        for ref, rep in ((near_ref, rep_pos), (far_ref, 1 - rep_pos)):
            begin = pl.multiple_of((at + rep) * piece, piece)
            ref[d] = acc_ref[pl.ds(begin, piece), :].astype(ref.dtype)


def merge_kernel(near_ref, far_ref, *out_refs):
    for d, ref in enumerate(out_refs):
        ref[...] = (near_ref[d] + far_ref[d].astype(F32)).astype(ref.dtype)


def finish_kernel(rows, *args):
    own, other, args = args[:rows], args[rows : 2 * rows], args[2 * rows :]
    terms, (source_out, target_out, sum_ref, sems) = args[:-4], args[-4:]
    rep_pos = lax.axis_index("rep")
    row_pos = lax.axis_index("row")
    piece = own[0].shape[0]
    per_tile = HALF // piece
    copies = []
    for refs, rep in ((own, rep_pos), (other, 1 - rep_pos)):
        for k, ref in enumerate(refs):
            at = row_pos ^ k
            begin = (at // per_tile) * TILE + rep * HALF + (at % per_tile) * piece
            copies.append(
                pltpu.make_async_copy(
                    ref,
                    target_out.at[pl.ds(pl.multiple_of(begin, piece), piece)],
                    sems.at[len(copies)],
                )
            )
    for copy in copies:
        copy.start()
    value = terms[0][...]
    for term in terms[1:]:
        value = value + term[...].astype(F32)
    sum_ref[...] = value.astype(sum_ref.dtype)
    copies.append(pltpu.make_async_copy(sum_ref, source_out, sems.at[len(copies)]))
    copies[-1].start()
    for copy in copies:
        copy.wait()


def call(kernel, name, outs, scratch, args, spaces=None, aliases=None, cost=None):
    spaces = spaces or [pltpu.VMEM] * len(args)
    args = [
        pltpu.with_memory_space_constraint(value, space)
        for value, space in zip(args, spaces)
    ]
    return pl.pallas_call(
        kernel,
        name=name,
        out_shape=[pltpu.VMEM(shape, dtype) for shape, dtype in outs],
        in_specs=[pl.BlockSpec(memory_space=space) for space in spaces],
        out_specs=[pl.BlockSpec(memory_space=pltpu.VMEM) for _ in outs],
        scratch_shapes=scratch,
        input_output_aliases=aliases or {},
        cost_estimate=cost,
        compiler_params=pltpu.CompilerParams(vmem_limit_bytes=LIMIT),
    )(*args)


def shards(
    sizes,
    source_emb,
    target_emb,
    warm_start,
    source_weight,
    target_weight,
    source_bounds,
    target_bounds,
    kept_pairs,
):
    width = source_emb.shape[1]

    def swap(value, axes, k):
        count = math.prod(sizes[axis] for axis in axes)
        return lax.ppermute(value, axes, [(i, i ^ k) for i in range(count)])

    def spread(value, axes):
        count = math.prod(sizes[axis] for axis in axes)
        return [value] + [swap(value, axes, k) for k in range(1, count)]

    bf16 = jnp.bfloat16
    over_source = ("col", "rep")
    over_target = ("row",)
    target_weight = target_weight.reshape(2 * BLOCK, 1, HALF)
    source_weight = source_weight.reshape(BLOCK, 1, TILE)
    source_vector = ((BLOCK, 1, TILE), F32)
    target_vector = ((BLOCK, 1, HALF), F32)
    matrix = (BLOCK, TILE, BLOCK * HALF)
    columns = (BLOCK, TILE, LANES)
    hbm = pltpu.HBM

    score, packed, meta, x, y, warm = call(
        first_source_kernel,
        "first_source",
        [
            (matrix, F32),
            ((2 * BLOCK, 1, TILE), F32),
            ((8, LANES), jnp.int32),
            ((BLOCK * TILE, width), bf16),
            ((BLOCK * HALF, width), bf16),
            target_vector,
        ],
        [
            pltpu.SMEM(source_bounds.shape, jnp.int32),
            pltpu.SMEM(target_bounds.shape, jnp.int32),
            pltpu.SMEM(kept_pairs.shape[::-1], jnp.int32),
        ]
        + [pltpu.SemaphoreType.DMA((BLOCK,))] * 4,
        [
            source_emb,
            target_emb,
            warm_start.reshape(2 * BLOCK, 1, HALF),
            source_bounds,
            target_bounds,
            kept_pairs.T,
        ],
        [hbm] * 6,
    )
    parts = spread(packed, over_source)
    n_source = len(parts)
    e, packed = call(
        functools.partial(first_target_kernel, n_source),
        "first_target",
        [(matrix, F32), ((2 * BLOCK, 1, HALF), F32)],
        [pltpu.VMEM(columns, F32)],
        [*parts, score, meta],
    )
    parts = spread(packed, over_target)
    n_target = len(parts)
    sums, q, wq = call(
        functools.partial(second_source_kernel, n_target),
        "second_source",
        [source_vector, target_vector, target_vector],
        [],
        [*parts, warm, e, meta],
    )
    parts = spread(sums, over_source)
    sums, a, a_column = call(
        functools.partial(second_target_kernel, n_source),
        "second_target",
        [target_vector, source_vector, (columns, F32)],
        [],
        [*parts, e, meta, q],
    )
    parts = spread(sums, over_target)
    sums, p = call(
        functools.partial(late_kernel, n_target),
        "late",
        [source_vector, target_vector],
        [],
        [*parts, e, meta, q, target_weight],
    )
    parts = spread(sums, over_source)
    sums, b_column = call(
        functools.partial(mid_kernel, n_source),
        "mid",
        [target_vector, (columns, F32)],
        [],
        [*parts, e, meta, q, a, source_weight],
    )
    parts = spread(sums, over_target)
    sums, h = call(
        functools.partial(early_kernel, n_target),
        "early",
        [source_vector, target_vector],
        [],
        [*parts, e, meta, q],
    )
    parts = spread(sums, over_source)

    rows = sizes["row"]
    per_tile = rows // BLOCK
    piece = HALF // per_tile
    shared = [x, e, meta, a_column, b_column, p, q, h, wq]
    pieces = [None] * rows
    arrived = [None] * rows
    bar = early = None
    for part in (2, 1, 3, 0):
        outs = [((piece, width), bf16 if part or i else F32) for i in range(per_tile)]
        if bar is None:
            bar, early, *results = call(
                functools.partial(target_gradient_kernel, part, n_source),
                f"target_gradient_{part}",
                [(matrix, bf16), (columns, F32)] + outs,
                [],
                [*parts, *shared],
            )
        else:
            bar, *results = call(
                functools.partial(target_gradient_kernel, part, 0),
                f"target_gradient_{part}",
                [(matrix, bf16)] + outs,
                [],
                [*shared, early, bar],
                aliases={len(shared) + 1: 0},
            )
        for i, value in enumerate(results):
            k = part * per_tile + i
            pieces[k] = value
            arrived[k] = swap(value, over_target, k) if k else value
    source_piece = BLOCK * TILE // n_source
    columns_of_chips = sizes["col"]
    halves = (columns_of_chips, source_piece, width)
    near, far = call(
        source_gradient_kernel,
        "source_gradient",
        [(halves, F32), (halves, bf16)],
        [pltpu.VMEM((BLOCK * TILE, width), F32)],
        [bar, y],
    )
    def added(values):
        value = values[0].astype(F32)
        for other in values[1:]:
            value = value + other.astype(F32)
        return value.astype(bf16)

    arrived, far = lax.optimization_barrier((arrived, far))
    target_rows = added(arrived)
    merged = call(
        merge_kernel,
        "merge",
        [((source_piece, width), bf16 if d else F32) for d in range(columns_of_chips)],
        [],
        [near, swap(far, ("rep",), 1)],
    )
    terms = [merged[0]] + [swap(merged[d], ("col",), d) for d in range(1, columns_of_chips)]
    gathered = spread(target_rows, over_target)
    gathered = gathered + [swap(value, ("rep",), 1) for value in gathered]
    source_shape = (source_piece, width)
    return pl.pallas_call(
        functools.partial(finish_kernel, rows),
        name="finish",
        out_shape=[
            jax.ShapeDtypeStruct(source_shape, bf16),
            jax.ShapeDtypeStruct(target_emb.shape, bf16),
        ],
        in_specs=[pl.BlockSpec(memory_space=pltpu.VMEM)] * (len(gathered) + len(terms)),
        out_specs=[pl.BlockSpec(memory_space=pltpu.HBM)] * 2,
        scratch_shapes=[
            pltpu.VMEM(source_shape, bf16),
            pltpu.SemaphoreType.DMA((len(gathered) + 1,)),
        ],
        compiler_params=pltpu.CompilerParams(vmem_limit_bytes=LIMIT),
    )(*gathered, *terms)


def solution(mesh):
    return jax.shard_map(
        functools.partial(shards, dict(mesh.shape)),
        mesh=mesh,
        in_specs=(
            P(("groups", "row"), None),
            P(("groups", "col"), None),
            P(("groups", "col")),
            P(("groups", "row")),
            P(("groups", "col")),
            P("groups"),
            P("groups"),
            P("groups", None),
        ),
        out_specs=(P(("groups", "row", "col", "rep"), None), P(("groups", "col"), None)),
        check_vma=False,
    )
```

```python
import functools
import math

import jax
import jax.numpy as jnp
from jax import lax
from jax.experimental import pallas as pl
from jax.experimental.pallas import tpu as pltpu
from jax.sharding import PartitionSpec as P

TILE = 512
HALF = 256
BLOCK = 4
LANES = 128
ROWS = 64
LIMIT = 24 * 1024 * 1024
LOWEST = -1e30
F32 = jnp.float32
NT_DIMS = (((1,), (1,)), ((), ()))
NN_DIMS = (((1,), (0,)), ((), ()))
TN_DIMS = (((0,), (0,)), ((), ()))


def kept_targets(meta, s):
    first_cut, second_cut, straight = meta
    is_low = (s < first_cut).astype(jnp.int32) == straight
    return jnp.where(is_low, 0, second_cut), jnp.where(is_low, second_cut, BLOCK)


def kept_sources(meta, t):
    first_cut, second_cut, straight = meta
    is_low = (t < second_cut).astype(jnp.int32) == straight
    return jnp.where(is_low, 0, first_cut), jnp.where(is_low, first_cut, BLOCK)


def tile_lanes(t):
    return pl.ds(pl.multiple_of(t * HALF, HALF), HALF)


def read_meta(meta_ref):
    return meta_ref[0, 0], meta_ref[0, 1], meta_ref[0, 2]


def to_column(row):
    return jnp.broadcast_to(row, (LANES, row.shape[1])).T


def lane_sums(values):
    return jnp.sum(values.T, axis=0, keepdims=True)


def total(refs, index):
    value = refs[0][index]
    for ref in refs[1:]:
        value = value + ref[index]
    return value


def for_widths(low, high, body):
    for n in range(1, BLOCK):
        pl.when(high - low == n)(functools.partial(body, n))


def weighted_rows(e_ref, meta, vector_ref, out_ref):
    def one(s, carry):
        low, high = kept_targets(meta, s)

        def body(n):
            vectors = [vector_ref[low + i] for i in range(n)]
            for at in range(0, TILE, LANES):
                acc = None
                for i in range(n):
                    e = e_ref[s, at : at + LANES, tile_lanes(low + i)]
                    term = e[:, :LANES] * vectors[i][:, :LANES] + e[:, LANES:] * vectors[i][:, LANES:]
                    acc = term if acc is None else acc + term
                out_ref[s, :, at : at + LANES] = lane_sums(acc)

        for_widths(low, high, body)
        return carry

    lax.fori_loop(0, BLOCK, one, 0)


def eight_rows(values, reduce):
    return reduce(values.reshape(-1, 8, LANES), axis=0)


def weighted_columns(e_ref, meta, column_ref, scale_ref, out_ref):
    def one(t, carry):
        low, high = kept_sources(meta, t)

        def step(s, acc):
            left, right = acc
            for at in range(0, TILE, ROWS):
                e = e_ref[s, at : at + ROWS, tile_lanes(t)]
                u = column_ref[s, at : at + ROWS, :]
                left = left + eight_rows(e[:, :LANES] * u, jnp.sum)
                right = right + eight_rows(e[:, LANES:] * u, jnp.sum)
            return left, right

        zero = jnp.zeros((8, LANES), F32)
        left, right = lax.fori_loop(low, high, step, (zero, zero))
        scale = scale_ref[t]
        out_ref[t, :, :LANES] = scale[:, :LANES] * jnp.sum(left, axis=0, keepdims=True)
        out_ref[t, :, LANES:] = scale[:, LANES:] * jnp.sum(right, axis=0, keepdims=True)
        return carry

    lax.fori_loop(0, BLOCK, one, 0)


def first_source_kernel(
    x_hbm,
    y_hbm,
    warm_hbm,
    sb_hbm,
    tb_hbm,
    kp_hbm,
    score_ref,
    out_ref,
    meta_ref,
    x_ref,
    y_ref,
    warm_ref,
    sb_ref,
    tb_ref,
    kp_ref,
    even_ref,
    odd_ref,
    x_sems,
    y_sems,
    warm_sems,
    bound_sems,
):
    row_pos = lax.axis_index("row")
    col_pos = lax.axis_index("col")
    rep_pos = lax.axis_index("rep")
    bounds = [
        pltpu.make_async_copy(source, target, bound_sems.at[i])
        for i, (source, target) in enumerate(
            ((sb_hbm, sb_ref), (tb_hbm, tb_ref), (kp_hbm, kp_ref))
        )
    ]
    x_copies, y_copies, warm_copies = [], [], []
    for t in range(BLOCK):
        begin = pl.multiple_of(t * TILE + rep_pos * HALF, HALF)
        y_copies.append(
            pltpu.make_async_copy(
                y_hbm.at[pl.ds(begin, HALF)], y_ref.at[pl.ds(t * HALF, HALF)], y_sems.at[t]
            )
        )
        warm_copies.append(
            pltpu.make_async_copy(warm_hbm.at[2 * t + rep_pos], warm_ref.at[t], warm_sems.at[t])
        )
        x_copies.append(
            pltpu.make_async_copy(
                x_hbm.at[pl.ds(t * TILE, TILE)], x_ref.at[pl.ds(t * TILE, TILE)], x_sems.at[t]
            )
        )
    for copy in bounds + y_copies + x_copies[:1] + warm_copies + x_copies[1:]:
        copy.start()
    for copy in bounds:
        copy.wait()
    first_cut = sb_ref[2 * row_pos + 1] - BLOCK * row_pos
    second_cut = tb_ref[2 * col_pos + 1] - BLOCK * col_pos

    def look(i, found):
        here = (kp_ref[0, i] == 2 * row_pos) & (kp_ref[1, i] == 2 * col_pos)
        return found | here.astype(jnp.int32)

    straight = lax.fori_loop(0, kp_ref.shape[1], look, jnp.int32(0))
    lanes = lax.broadcasted_iota(jnp.int32, meta_ref.shape, 1)
    meta_ref[...] = jnp.where(lanes == 0, first_cut, jnp.where(lanes == 1, second_cut, straight))
    meta = (first_cut, second_cut, straight)
    inv_root = x_ref.shape[1] ** (-0.5)
    for copy in y_copies:
        copy.wait()

    def scores(s):
        buffers[s % 2][...] = inv_root * lax.dot_general(
            x_ref[s * TILE : (s + 1) * TILE, :],
            y_ref[...],
            NT_DIMS,
            preferred_element_type=F32,
        )

    buffers = (even_ref, odd_ref)
    x_copies[0].wait()
    scores(0)
    for copy in warm_copies:
        copy.wait()
    for s in range(BLOCK):
        low, high = kept_targets(meta, s)
        buffer = buffers[s % 2]
        if s + 1 < BLOCK:
            x_copies[s + 1].wait()

        def body(n):
            warm = [warm_ref[low + i] for i in range(n)]
            if s + 1 < BLOCK:
                scores(s + 1)
            for at in range(0, TILE, LANES):
                largest = None
                for i in range(n):
                    e = buffer[at : at + LANES, tile_lanes(low + i)]
                    score_ref[s, at : at + LANES, tile_lanes(low + i)] = e
                    term = jnp.maximum(
                        e[:, :LANES] + warm[i][:, :LANES], e[:, LANES:] + warm[i][:, LANES:]
                    )
                    largest = term if largest is None else jnp.maximum(largest, term)
                largest = jnp.max(largest, axis=1, keepdims=True)
                largest = jnp.broadcast_to(largest, (LANES, LANES))
                acc = None
                for i in range(n):
                    e = buffer[at : at + LANES, tile_lanes(low + i)]
                    term = jnp.exp(e[:, :LANES] + warm[i][:, :LANES] - largest) + jnp.exp(
                        e[:, LANES:] + warm[i][:, LANES:] - largest
                    )
                    acc = term if acc is None else acc + term
                out_ref[s, :, at : at + LANES] = largest.T[:1]
                out_ref[BLOCK + s, :, at : at + LANES] = lane_sums(acc)

        for_widths(low, high, body)


def combine(refs, at, offset):
    largest = refs[0][at]
    for ref in refs[1:]:
        largest = jnp.maximum(largest, ref[at])
    sums = refs[0][offset + at] * jnp.exp(refs[0][at] - largest)
    for ref in refs[1:]:
        sums = sums + ref[offset + at] * jnp.exp(ref[at] - largest)
    return -(largest + jnp.log(sums))


def first_target_kernel(count, *args):
    parts = args[:count]
    score_ref, meta_ref, e_ref, out_ref, column_ref = args[count:]
    meta = read_meta(meta_ref)
    for s in range(BLOCK):
        column_ref[s] = to_column(combine(parts, s, BLOCK))

    def one(t, carry):
        low, high = kept_sources(meta, t)

        def peak(s, acc):
            left, right = acc
            for at in range(0, TILE, ROWS):
                e = score_ref[s, at : at + ROWS, tile_lanes(t)]
                u = column_ref[s, at : at + ROWS, :]
                left = jnp.maximum(left, eight_rows(e[:, :LANES] + u, jnp.max))
                right = jnp.maximum(right, eight_rows(e[:, LANES:] + u, jnp.max))
            return left, right

        lowest = jnp.full((8, LANES), LOWEST, F32)
        left, right = lax.fori_loop(low, high, peak, (lowest, lowest))
        left = jnp.max(left, axis=0, keepdims=True)
        right = jnp.max(right, axis=0, keepdims=True)
        out_ref[t, :, :LANES] = left
        out_ref[t, :, LANES:] = right

        def step(s, acc):
            left_sum, right_sum = acc
            for at in range(0, TILE, ROWS):
                e = score_ref[s, at : at + ROWS, tile_lanes(t)]
                u = column_ref[s, at : at + ROWS, :]
                e_left = jnp.exp(e[:, :LANES] + u - left)
                e_right = jnp.exp(e[:, LANES:] + u - right)
                e_ref[s, at : at + ROWS, tile_lanes(t)] = jnp.concatenate([e_left, e_right], axis=1)
                left_sum = left_sum + eight_rows(e_left, jnp.sum)
                right_sum = right_sum + eight_rows(e_right, jnp.sum)
            return left_sum, right_sum

        zero = jnp.zeros((8, LANES), F32)
        left_sum, right_sum = lax.fori_loop(low, high, step, (zero, zero))
        out_ref[BLOCK + t, :, :LANES] = jnp.sum(left_sum, axis=0, keepdims=True)
        out_ref[BLOCK + t, :, LANES:] = jnp.sum(right_sum, axis=0, keepdims=True)
        return carry

    lax.fori_loop(0, BLOCK, one, 0)


def second_source_kernel(count, *args):
    parts = args[:count]
    warm_ref, e_ref, meta_ref, out_ref, q_ref, wq_ref = args[count:]
    for t in range(BLOCK):
        potential = combine(parts, t, BLOCK)
        q = jnp.exp(parts[0][t] + potential)
        q_ref[t] = q
        wq_ref[t] = q * jnp.exp(warm_ref[t] - potential)
    weighted_rows(e_ref, read_meta(meta_ref), q_ref, out_ref)


def second_target_kernel(count, *args):
    parts = args[:count]
    e_ref, meta_ref, q_ref, out_ref, a_ref, column_ref = args[count:]
    for s in range(BLOCK):
        a = 1.0 / total(parts, s)
        a_ref[s] = a
        column_ref[s] = to_column(a)
    weighted_columns(e_ref, read_meta(meta_ref), column_ref, q_ref, out_ref)


def late_kernel(count, *args):
    parts = args[:count]
    e_ref, meta_ref, q_ref, weight_ref, out_ref, p_ref = args[count:]
    rep_pos = lax.axis_index("rep")
    for t in range(BLOCK):
        p_ref[t] = weight_ref[2 * t + rep_pos] * q_ref[t] / total(parts, t)
    weighted_rows(e_ref, read_meta(meta_ref), p_ref, out_ref)


def mid_kernel(count, *args):
    parts = args[:count]
    e_ref, meta_ref, q_ref, a_ref, weight_ref, out_ref, column_ref = args[count:]
    for s in range(BLOCK):
        a = a_ref[s]
        column_ref[s] = to_column(a * (weight_ref[s] - a * total(parts, s)))
    weighted_columns(e_ref, read_meta(meta_ref), column_ref, q_ref, out_ref)


def early_kernel(count, *args):
    parts = args[:count]
    e_ref, meta_ref, q_ref, out_ref, h_ref = args[count:]
    for t in range(BLOCK):
        h_ref[t] = -q_ref[t] * total(parts, t)
    weighted_rows(e_ref, read_meta(meta_ref), h_ref, out_ref)


def target_gradient_kernel(part, count, *args):
    if count:
        parts = args[:count]
        x_ref, e_ref, meta_ref, a_ref, b_ref, p_ref, q_ref, h_ref, wq_ref = args[count : count + 9]
        bar_ref, early_ref, *out_refs = args[count + 9 :]
        for s in range(BLOCK):
            early_ref[s] = to_column(-total(parts, s))
    else:
        x_ref, e_ref, meta_ref, a_ref, b_ref, p_ref, q_ref, h_ref, wq_ref = args[:9]
        early_ref, _, bar_ref, *out_refs = args[9:]
    row_pos = lax.axis_index("row")
    per_tile = len(out_refs)
    t = (row_pos // per_tile) ^ part
    low, high = kept_sources(read_meta(meta_ref), t)
    p, q, h, wq = p_ref[t], q_ref[t], h_ref[t], wq_ref[t]
    inv_root = x_ref.shape[1] ** (-0.5)
    piece = HALF // per_tile

    def term(s):
        for at in range(0, TILE, ROWS):
            e = e_ref[s, at : at + ROWS, tile_lanes(t)]
            a = a_ref[s, at : at + ROWS, :]
            b = b_ref[s, at : at + ROWS, :]
            early = early_ref[s, at : at + ROWS, :]
            sides = []
            for side in (slice(0, LANES), slice(LANES, HALF)):
                factor = a * p[:, side] + b * q[:, side] + (h[:, side] + early * wq[:, side])
                sides.append((e[:, side] * factor).astype(jnp.bfloat16))
            bar_ref[s, at : at + ROWS, tile_lanes(t)] = jnp.concatenate(sides, axis=1)
        x = x_ref[pl.ds(pl.multiple_of(s * TILE, TILE), TILE), :]
        bar = bar_ref[s, :, tile_lanes(t)]
        return lax.dot_general(bar, x, TN_DIMS, preferred_element_type=F32)

    def body(n):
        result = term(low)
        for i in range(1, n):
            result = result + term(low + i)
        result = -inv_root * result
        for i, ref in enumerate(out_refs):
            for j in range(per_tile):

                @pl.when(((row_pos % per_tile) ^ i) == j)
                def _():
                    ref[...] = result[j * piece : (j + 1) * piece, :].astype(ref.dtype)

    for_widths(low, high, body)


def source_gradient_kernel(bar_ref, y_ref, meta_ref, near_ref, far_ref, acc_ref):
    inv_root = y_ref.shape[1] ** (-0.5)
    col_pos = lax.axis_index("col")
    rep_pos = lax.axis_index("rep")
    meta = read_meta(meta_ref)
    for s in range(BLOCK):
        low, high = kept_targets(meta, s)

        def body(n):
            kept = pl.ds(pl.multiple_of(low * HALF, HALF), n * HALF)
            acc_ref[s * TILE : (s + 1) * TILE, :] = -inv_root * lax.dot_general(
                bar_ref[s, :, kept], y_ref[kept, :], NN_DIMS, preferred_element_type=F32
            )

        for_widths(low, high, body)
    piece = near_ref.shape[1]
    for d in range(near_ref.shape[0]):
        at = 2 * (col_pos ^ d)
        for ref, rep in ((near_ref, rep_pos), (far_ref, 1 - rep_pos)):
            begin = pl.multiple_of((at + rep) * piece, piece)
            ref[d] = acc_ref[pl.ds(begin, piece), :].astype(ref.dtype)


def merge_kernel(near_ref, far_ref, *out_refs):
    for d, ref in enumerate(out_refs):
        ref[...] = (near_ref[d] + far_ref[d].astype(F32)).astype(ref.dtype)


def finish_kernel(rows, *args):
    own, other, args = args[:rows], args[rows : 2 * rows], args[2 * rows :]
    terms, (source_out, target_out, sum_ref, sems) = args[:-4], args[-4:]
    rep_pos = lax.axis_index("rep")
    row_pos = lax.axis_index("row")
    piece = own[0].shape[0]
    per_tile = HALF // piece
    copies = []
    for refs, rep in ((own, rep_pos), (other, 1 - rep_pos)):
        for k, ref in enumerate(refs):
            at = row_pos ^ k
            begin = (at // per_tile) * TILE + rep * HALF + (at % per_tile) * piece
            copies.append(
                pltpu.make_async_copy(
                    ref,
                    target_out.at[pl.ds(pl.multiple_of(begin, piece), piece)],
                    sems.at[len(copies)],
                )
            )
    for copy in copies:
        copy.start()
    value = terms[0][...]
    for term in terms[1:]:
        value = value + term[...].astype(F32)
    sum_ref[...] = value.astype(sum_ref.dtype)
    copies.append(pltpu.make_async_copy(sum_ref, source_out, sems.at[len(copies)]))
    copies[-1].start()
    for copy in copies:
        copy.wait()


def call(kernel, name, outs, scratch, args, spaces=None, aliases=None, cost=None):
    spaces = spaces or [pltpu.VMEM] * len(args)
    args = [
        pltpu.with_memory_space_constraint(value, space)
        for value, space in zip(args, spaces)
    ]
    return pl.pallas_call(
        kernel,
        name=name,
        out_shape=[pltpu.VMEM(shape, dtype) for shape, dtype in outs],
        in_specs=[pl.BlockSpec(memory_space=space) for space in spaces],
        out_specs=[pl.BlockSpec(memory_space=pltpu.VMEM) for _ in outs],
        scratch_shapes=scratch,
        input_output_aliases=aliases or {},
        cost_estimate=cost,
        compiler_params=pltpu.CompilerParams(vmem_limit_bytes=LIMIT),
    )(*args)


def shards(
    sizes,
    source_emb,
    target_emb,
    warm_start,
    source_weight,
    target_weight,
    source_bounds,
    target_bounds,
    kept_pairs,
):
    width = source_emb.shape[1]

    def swap(value, axes, k):
        count = math.prod(sizes[axis] for axis in axes)
        return lax.ppermute(value, axes, [(i, i ^ k) for i in range(count)])

    def spread(value, axes):
        count = math.prod(sizes[axis] for axis in axes)
        return [value] + [swap(value, axes, k) for k in range(1, count)]

    bf16 = jnp.bfloat16
    over_source = ("col", "rep")
    over_target = ("row",)
    target_weight = target_weight.reshape(2 * BLOCK, 1, HALF)
    source_weight = source_weight.reshape(BLOCK, 1, TILE)
    source_vector = ((BLOCK, 1, TILE), F32)
    target_vector = ((BLOCK, 1, HALF), F32)
    matrix = (BLOCK, TILE, BLOCK * HALF)
    columns = (BLOCK, TILE, LANES)
    hbm = pltpu.HBM

    score, packed, meta, x, y, warm = call(
        first_source_kernel,
        "first_source",
        [
            (matrix, F32),
            ((2 * BLOCK, 1, TILE), F32),
            ((8, LANES), jnp.int32),
            ((BLOCK * TILE, width), bf16),
            ((BLOCK * HALF, width), bf16),
            target_vector,
        ],
        [
            pltpu.SMEM(source_bounds.shape, jnp.int32),
            pltpu.SMEM(target_bounds.shape, jnp.int32),
            pltpu.SMEM(kept_pairs.shape[::-1], jnp.int32),
            pltpu.VMEM(matrix[1:], F32),
            pltpu.VMEM(matrix[1:], F32),
        ]
        + [pltpu.SemaphoreType.DMA((BLOCK,))] * 4,
        [
            source_emb,
            target_emb,
            warm_start.reshape(2 * BLOCK, 1, HALF),
            source_bounds,
            target_bounds,
            kept_pairs.T,
        ],
        [hbm] * 6,
    )
    parts = spread(packed, over_source)
    n_source = len(parts)
    e, packed = call(
        functools.partial(first_target_kernel, n_source),
        "first_target",
        [(matrix, F32), ((2 * BLOCK, 1, HALF), F32)],
        [pltpu.VMEM(columns, F32)],
        [*parts, score, meta],
    )
    parts = spread(packed, over_target)
    n_target = len(parts)
    sums, q, wq = call(
        functools.partial(second_source_kernel, n_target),
        "second_source",
        [source_vector, target_vector, target_vector],
        [],
        [*parts, warm, e, meta],
    )
    parts = spread(sums, over_source)
    sums, a, a_column = call(
        functools.partial(second_target_kernel, n_source),
        "second_target",
        [target_vector, source_vector, (columns, F32)],
        [],
        [*parts, e, meta, q],
    )
    parts = spread(sums, over_target)
    sums, p = call(
        functools.partial(late_kernel, n_target),
        "late",
        [source_vector, target_vector],
        [],
        [*parts, e, meta, q, target_weight],
    )
    parts = spread(sums, over_source)
    sums, b_column = call(
        functools.partial(mid_kernel, n_source),
        "mid",
        [target_vector, (columns, F32)],
        [],
        [*parts, e, meta, q, a, source_weight],
    )
    parts = spread(sums, over_target)
    sums, h = call(
        functools.partial(early_kernel, n_target),
        "early",
        [source_vector, target_vector],
        [],
        [*parts, e, meta, q],
    )
    parts = spread(sums, over_source)

    rows = sizes["row"]
    per_tile = rows // BLOCK
    piece = HALF // per_tile
    shared = [x, e, meta, a_column, b_column, p, q, h, wq]
    pieces = [None] * rows
    arrived = [None] * rows
    bar = early = None
    for part in (3, 2, 1, 0):
        outs = [((piece, width), bf16 if part or i else F32) for i in range(per_tile)]
        if bar is None:
            bar, early, *results = call(
                functools.partial(target_gradient_kernel, part, n_source),
                f"target_gradient_{part}",
                [(matrix, bf16), (columns, F32)] + outs,
                [],
                [*parts, *shared],
            )
        else:
            if part == 0:
                first = slice((3, 2, 1, 0)[0] * per_tile, ((3, 2, 1, 0)[0] + 1) * per_tile)
                bar, arrived[first] = lax.optimization_barrier((bar, arrived[first]))
            bar, *results = call(
                functools.partial(target_gradient_kernel, part, 0),
                f"target_gradient_{part}",
                [(matrix, bf16)] + outs,
                [],
                [*shared, early, bar],
                aliases={len(shared) + 1: 0},
            )
        for i, value in enumerate(results):
            k = part * per_tile + i
            pieces[k] = value
            arrived[k] = swap(value, over_target, k) if k else value
    source_piece = BLOCK * TILE // n_source
    columns_of_chips = sizes["col"]
    halves = (columns_of_chips, source_piece, width)
    near, far = call(
        source_gradient_kernel,
        "source_gradient",
        [(halves, F32), (halves, bf16)],
        [pltpu.VMEM((BLOCK * TILE, width), F32)],
        [bar, y, meta],
    )
    def added(values):
        value = values[0].astype(F32)
        for other in values[1:]:
            value = value + other.astype(F32)
        return value.astype(bf16)

    arrived, far = lax.optimization_barrier((arrived, far))
    target_rows = added(arrived)
    merged = call(
        merge_kernel,
        "merge",
        [((source_piece, width), bf16 if d else F32) for d in range(columns_of_chips)],
        [],
        [near, swap(far, ("rep",), 1)],
    )
    terms = [merged[0]] + [swap(merged[d], ("col",), d) for d in range(1, columns_of_chips)]
    gathered = spread(target_rows, over_target)
    gathered = gathered + [swap(value, ("rep",), 1) for value in gathered]
    source_shape = (source_piece, width)
    return pl.pallas_call(
        functools.partial(finish_kernel, rows),
        name="finish",
        out_shape=[
            jax.ShapeDtypeStruct(source_shape, bf16),
            jax.ShapeDtypeStruct(target_emb.shape, bf16),
        ],
        in_specs=[pl.BlockSpec(memory_space=pltpu.VMEM)] * (len(gathered) + len(terms)),
        out_specs=[pl.BlockSpec(memory_space=pltpu.HBM)] * 2,
        scratch_shapes=[
            pltpu.VMEM(source_shape, bf16),
            pltpu.SemaphoreType.DMA((len(gathered) + 1,)),
        ],
        compiler_params=pltpu.CompilerParams(vmem_limit_bytes=LIMIT),
    )(*gathered, *terms)


def solution(mesh):
    return jax.shard_map(
        functools.partial(shards, dict(mesh.shape)),
        mesh=mesh,
        in_specs=(
            P(("groups", "row"), None),
            P(("groups", "col"), None),
            P(("groups", "col")),
            P(("groups", "row")),
            P(("groups", "col")),
            P("groups"),
            P("groups"),
            P("groups", None),
        ),
        out_specs=(P(("groups", "row", "col", "rep"), None), P(("groups", "col"), None)),
        check_vma=False,
    )
```

```python
import functools
import math

import jax
import jax.numpy as jnp
from jax import lax
from jax.experimental import pallas as pl
from jax.experimental.pallas import tpu as pltpu
from jax.sharding import PartitionSpec as P

TILE = 512
HALF = 256
BLOCK = 4
LANES = 128
ROWS = 64
LIMIT = 24 * 1024 * 1024
LOWEST = -1e30
F32 = jnp.float32
NT_DIMS = (((1,), (1,)), ((), ()))
NN_DIMS = (((1,), (0,)), ((), ()))
TN_DIMS = (((0,), (0,)), ((), ()))


def kept_targets(meta, s):
    first_cut, second_cut, straight = meta
    is_low = (s < first_cut).astype(jnp.int32) == straight
    return jnp.where(is_low, 0, second_cut), jnp.where(is_low, second_cut, BLOCK)


def kept_sources(meta, t):
    first_cut, second_cut, straight = meta
    is_low = (t < second_cut).astype(jnp.int32) == straight
    return jnp.where(is_low, 0, first_cut), jnp.where(is_low, first_cut, BLOCK)


def tile_lanes(t):
    return pl.ds(pl.multiple_of(t * HALF, HALF), HALF)


def read_meta(meta_ref):
    return meta_ref[0, 0], meta_ref[0, 1], meta_ref[0, 2]


def to_column(row):
    return jnp.broadcast_to(row, (LANES, row.shape[1])).T


def lane_sums(values):
    return jnp.sum(values.T, axis=0, keepdims=True)


def total(refs, index):
    value = refs[0][index]
    for ref in refs[1:]:
        value = value + ref[index]
    return value


def tile_biases(meta, s):
    low, high = kept_targets(meta, s)
    return [jnp.where((low <= t) & (t < high), 0.0, LOWEST) for t in range(BLOCK)]


def lane_groups():
    return [(i // 2, slice(i * LANES, (i + 1) * LANES)) for i in range(2 * BLOCK)]


def half_of(i):
    return slice((i % 2) * LANES, (i % 2 + 1) * LANES)


def weighted_rows(e_ref, vector_ref, out_ref):
    for s in range(BLOCK):
        for at in range(0, TILE, LANES):
            acc = None
            for i, (t, lanes) in enumerate(lane_groups()):
                term = e_ref[s, at : at + LANES, lanes] * vector_ref[t, :, half_of(i)]
                acc = term if acc is None else acc + term
            out_ref[s, :, at : at + LANES] = lane_sums(acc)


def eight_rows(values, reduce):
    return reduce(values.reshape(-1, 8, LANES), axis=0)


def weighted_columns(e_ref, column_ref, scale_ref, out_ref):
    acc = [None] * (2 * BLOCK)
    for s in range(BLOCK):
        for at in range(0, TILE, LANES):
            u = column_ref[s, at : at + LANES, :]
            for i, (t, lanes) in enumerate(lane_groups()):
                term = eight_rows(e_ref[s, at : at + LANES, lanes] * u, jnp.sum)
                acc[i] = term if acc[i] is None else acc[i] + term
    for i, (t, lanes) in enumerate(lane_groups()):
        half = half_of(i)
        out_ref[t, :, half] = scale_ref[t, :, half] * jnp.sum(acc[i], axis=0, keepdims=True)


def first_source_kernel(
    x_hbm,
    y_hbm,
    warm_hbm,
    sb_hbm,
    tb_hbm,
    kp_hbm,
    score_ref,
    out_ref,
    meta_ref,
    x_ref,
    y_ref,
    warm_ref,
    sb_ref,
    tb_ref,
    kp_ref,
    sems,
    bound_sems,
):
    row_pos = lax.axis_index("row")
    col_pos = lax.axis_index("col")
    rep_pos = lax.axis_index("rep")
    bounds = [
        pltpu.make_async_copy(source, target, bound_sems.at[i])
        for i, (source, target) in enumerate(
            ((sb_hbm, sb_ref), (tb_hbm, tb_ref), (kp_hbm, kp_ref))
        )
    ]
    y_copy = pltpu.make_async_copy(y_hbm.at[:, rep_pos], y_ref, sems.at[0])
    x_copy = pltpu.make_async_copy(x_hbm.at[:1], x_ref.at[:1], sems.at[1])
    rest_copy = pltpu.make_async_copy(x_hbm.at[1:], x_ref.at[1:], sems.at[2])
    warm_copy = pltpu.make_async_copy(warm_hbm.at[:, rep_pos], warm_ref, sems.at[3])
    copies = [y_copy, x_copy, *bounds, warm_copy, rest_copy]
    for copy in copies:
        copy.start()
    for copy in bounds:
        copy.wait()
    first_cut = sb_ref[2 * row_pos + 1] - BLOCK * row_pos
    second_cut = tb_ref[2 * col_pos + 1] - BLOCK * col_pos

    def look(i, found):
        here = (kp_ref[0, i] == 2 * row_pos) & (kp_ref[1, i] == 2 * col_pos)
        return found | here.astype(jnp.int32)

    straight = lax.fori_loop(0, kp_ref.shape[1], look, jnp.int32(0))
    lanes = lax.broadcasted_iota(jnp.int32, meta_ref.shape, 1)
    meta_ref[...] = jnp.where(lanes == 0, first_cut, jnp.where(lanes == 1, second_cut, straight))
    meta = (first_cut, second_cut, straight)
    width = x_ref.shape[2]
    scale = width ** (-0.5) * math.log2(math.e)

    def scores(s):
        score_ref[s] = scale * lax.dot_general(
            x_ref[s],
            y_ref[...].reshape(BLOCK * HALF, width),
            NT_DIMS,
            preferred_element_type=F32,
        )

    def passes(s):
        biases = tile_biases(meta, s)
        warm = [
            warm_ref[t, :, half_of(i)] * math.log2(math.e) + biases[t]
            for i, (t, _) in enumerate(lane_groups())
        ]
        for at in range(0, TILE, LANES):
            largest = None
            for i, (_, lanes) in enumerate(lane_groups()):
                term = score_ref[s, at : at + LANES, lanes] + warm[i]
                largest = term if largest is None else jnp.maximum(largest, term)
            largest = jnp.max(largest, axis=1, keepdims=True)
            largest = jnp.broadcast_to(largest, (LANES, LANES))
            acc = None
            for i, (_, lanes) in enumerate(lane_groups()):
                term = jnp.exp2(score_ref[s, at : at + LANES, lanes] + warm[i] - largest)
                acc = term if acc is None else acc + term
            out_ref[s, :, at : at + LANES] = largest.T[:1]
            out_ref[BLOCK + s, :, at : at + LANES] = lane_sums(acc)

    y_copy.wait()
    x_copy.wait()
    scores(0)
    warm_copy.wait()
    rest_copy.wait()
    for s in range(BLOCK):
        if s + 1 < BLOCK:
            scores(s + 1)
        passes(s)


def combine(refs, at, offset):
    largest = refs[0][at]
    for ref in refs[1:]:
        largest = jnp.maximum(largest, ref[at])
    sums = refs[0][offset + at] * jnp.exp2(refs[0][at] - largest)
    for ref in refs[1:]:
        sums = sums + ref[offset + at] * jnp.exp2(ref[at] - largest)
    return -(largest + jnp.log2(sums))


def first_target_kernel(count, *args):
    parts = args[:count]
    score_ref, meta_ref, e_ref, out_ref, column_ref = args[count:]
    meta = read_meta(meta_ref)
    biases = [tile_biases(meta, s) for s in range(BLOCK)]
    largest = [None] * (2 * BLOCK)
    for s in range(BLOCK):
        column_ref[s] = to_column(combine(parts, s, BLOCK))
        here = [None] * (2 * BLOCK)
        for at in range(0, TILE, LANES):
            u = column_ref[s, at : at + LANES, :]
            for i, (t, lanes) in enumerate(lane_groups()):
                term = eight_rows(score_ref[s, at : at + LANES, lanes] + u, jnp.max)
                here[i] = term if here[i] is None else jnp.maximum(here[i], term)
        for i, (t, _) in enumerate(lane_groups()):
            term = here[i] + biases[s][t]
            largest[i] = term if s == 0 else jnp.maximum(largest[i], term)
    sums = [None] * (2 * BLOCK)
    for i, (t, _) in enumerate(lane_groups()):
        largest[i] = jnp.max(largest[i], axis=0, keepdims=True)
        out_ref[t, :, half_of(i)] = largest[i]
    for s in range(BLOCK):
        shifts = [largest[i] - biases[s][t] for i, (t, _) in enumerate(lane_groups())]
        for at in range(0, TILE, LANES):
            u = column_ref[s, at : at + LANES, :]
            for i, (t, lanes) in enumerate(lane_groups()):
                e = jnp.exp2(score_ref[s, at : at + LANES, lanes] + u - shifts[i])
                e_ref[s, at : at + LANES, lanes] = e
                term = eight_rows(e, jnp.sum)
                sums[i] = term if sums[i] is None else sums[i] + term
    for i, (t, _) in enumerate(lane_groups()):
        out_ref[BLOCK + t, :, half_of(i)] = jnp.sum(sums[i], axis=0, keepdims=True)


def second_source_kernel(count, *args):
    parts = args[:count]
    warm_ref, e_ref, out_ref, q_ref, wq_ref = args[count:]
    for t in range(BLOCK):
        potential = combine(parts, t, BLOCK)
        q = jnp.exp2(parts[0][t] + potential)
        q_ref[t] = q
        wq_ref[t] = q * jnp.exp2(warm_ref[t] * math.log2(math.e) - potential)
    weighted_rows(e_ref, q_ref, out_ref)


def second_target_kernel(count, *args):
    parts = args[:count]
    e_ref, q_ref, out_ref, a_ref, column_ref = args[count:]
    for s in range(BLOCK):
        a = 1.0 / total(parts, s)
        a_ref[s] = a
        column_ref[s] = to_column(a)
    weighted_columns(e_ref, column_ref, q_ref, out_ref)


def late_kernel(count, *args):
    parts = args[:count]
    e_ref, q_ref, weight_ref, out_ref, p_ref = args[count:]
    rep_pos = lax.axis_index("rep")
    for t in range(BLOCK):
        p_ref[t] = weight_ref[2 * t + rep_pos] * q_ref[t] / total(parts, t)
    weighted_rows(e_ref, p_ref, out_ref)


def mid_kernel(count, *args):
    parts = args[:count]
    e_ref, q_ref, a_ref, weight_ref, out_ref, column_ref = args[count:]
    for s in range(BLOCK):
        a = a_ref[s]
        column_ref[s] = to_column(a * (weight_ref[s] - a * total(parts, s)))
    weighted_columns(e_ref, column_ref, q_ref, out_ref)


def early_kernel(count, *args):
    parts = args[:count]
    e_ref, q_ref, out_ref, h_ref = args[count:]
    for t in range(BLOCK):
        h_ref[t] = -q_ref[t] * total(parts, t)
    weighted_rows(e_ref, h_ref, out_ref)


def target_gradient_kernel(part, count, *args):
    if count:
        parts = args[:count]
        x_ref, e_ref, a_ref, b_ref, p_ref, q_ref, h_ref, wq_ref = args[count : count + 8]
        bar_ref, early_ref, *out_refs = args[count + 8 :]
        for s in range(BLOCK):
            early_ref[s] = to_column(-total(parts, s))
    else:
        x_ref, e_ref, a_ref, b_ref, p_ref, q_ref, h_ref, wq_ref = args[:8]
        early_ref, _, bar_ref, *out_refs = args[8:]
    row_pos = lax.axis_index("row")
    per_tile = len(out_refs)
    t = (row_pos // per_tile) ^ part
    p, q, h, wq = p_ref[t], q_ref[t], h_ref[t], wq_ref[t]
    width = x_ref.shape[2]
    result = None
    for s in range(BLOCK):
        bars = []
        for at in range(0, TILE, ROWS):
            e = e_ref[s, at : at + ROWS, tile_lanes(t)]
            a = a_ref[s, at : at + ROWS, :]
            b = b_ref[s, at : at + ROWS, :]
            early = early_ref[s, at : at + ROWS, :]
            sides = []
            for side in (slice(0, LANES), slice(LANES, HALF)):
                factor = a * p[:, side] + b * q[:, side] + (h[:, side] + early * wq[:, side])
                sides.append((e[:, side] * factor).astype(jnp.bfloat16))
            bars.append(jnp.concatenate(sides, axis=1))
        bar = jnp.concatenate(bars, axis=0)
        bar_ref[s, :, tile_lanes(t)] = bar
        term = lax.dot_general(bar, x_ref[s], TN_DIMS, preferred_element_type=F32)
        result = term if result is None else result + term
    result = -(width ** (-0.5)) * result
    if per_tile == 1:
        out_refs[0][...] = result.astype(out_refs[0].dtype)
        return
    piece = HALF // per_tile
    for i, ref in enumerate(out_refs):
        for j in range(per_tile):

            @pl.when(((row_pos % per_tile) ^ i) == j)
            def _():
                ref[...] = result[j * piece : (j + 1) * piece, :].astype(ref.dtype)


def source_gradient_kernel(bar_ref, y_ref, near_ref, far_ref, acc_ref):
    width = y_ref.shape[2]
    col_pos = lax.axis_index("col")
    rep_pos = lax.axis_index("rep")
    y = y_ref[...].reshape(BLOCK * HALF, width)
    for s in range(BLOCK):
        acc_ref[s * TILE : (s + 1) * TILE, :] = -(width ** (-0.5)) * lax.dot_general(
            bar_ref[s], y, NN_DIMS, preferred_element_type=F32
        )
    piece = near_ref.shape[1]
    for d in range(near_ref.shape[0]):
        at = 2 * (col_pos ^ d)
        for ref, rep in ((near_ref, rep_pos), (far_ref, 1 - rep_pos)):
            begin = pl.multiple_of((at + rep) * piece, piece)
            ref[d] = acc_ref[pl.ds(begin, piece), :].astype(ref.dtype)


def merge_kernel(near_ref, far_ref, *out_refs):
    for d, ref in enumerate(out_refs):
        ref[...] = (near_ref[d] + far_ref[d].astype(F32)).astype(ref.dtype)


def finish_kernel(ranks, count, *args):
    pieces, args = args[: len(ranks)], args[len(ranks) :]
    terms, args = args[:count], args[count:]
    if terms:
        source_out, target_out, sum_ref, sems = args
    else:
        _, target_out, sems = args
    rep_pos = lax.axis_index("rep")
    row_pos = lax.axis_index("row")
    piece = pieces[0].shape[0]
    per_tile = HALF // piece
    copies = []
    for i, ((k, crossed), ref) in enumerate(zip(ranks, pieces)):
        at = row_pos ^ k
        rep = 1 - rep_pos if crossed else rep_pos
        begin = (at // per_tile) * TILE + rep * HALF + (at % per_tile) * piece
        begin = pl.multiple_of(begin, piece)
        copies.append(
            pltpu.make_async_copy(ref, target_out.at[pl.ds(begin, piece)], sems.at[i])
        )
    for copy in copies:
        copy.start()
    if terms:
        value = terms[0][...]
        for term in terms[1:]:
            value = value + term[...].astype(F32)
        sum_ref[...] = value.astype(sum_ref.dtype)
        copies.append(pltpu.make_async_copy(sum_ref, source_out, sems.at[len(ranks)]))
        copies[-1].start()
    for copy in copies:
        copy.wait()


def call(kernel, name, outs, scratch, args, spaces=None, aliases=None, cost=None):
    spaces = spaces or [pltpu.VMEM] * len(args)
    args = [
        pltpu.with_memory_space_constraint(value, space)
        for value, space in zip(args, spaces)
    ]
    return pl.pallas_call(
        kernel,
        name=name,
        out_shape=[pltpu.VMEM(shape, dtype) for shape, dtype in outs],
        in_specs=[pl.BlockSpec(memory_space=space) for space in spaces],
        out_specs=[pl.BlockSpec(memory_space=pltpu.VMEM) for _ in outs],
        scratch_shapes=scratch,
        input_output_aliases=aliases or {},
        cost_estimate=cost,
        compiler_params=pltpu.CompilerParams(vmem_limit_bytes=LIMIT),
    )(*args)


def shards(
    sizes,
    source_emb,
    target_emb,
    warm_start,
    source_weight,
    target_weight,
    source_bounds,
    target_bounds,
    kept_pairs,
):
    width = source_emb.shape[1]

    def swap(value, axes, k):
        count = math.prod(sizes[axis] for axis in axes)
        return lax.ppermute(value, axes, [(i, i ^ k) for i in range(count)])

    def spread(value, axes):
        count = math.prod(sizes[axis] for axis in axes)
        return [value] + [swap(value, axes, k) for k in range(1, count)]

    bf16 = jnp.bfloat16
    over_source = ("col", "rep")
    over_target = ("row",)
    target_weight = target_weight.reshape(2 * BLOCK, 1, HALF)
    source_weight = source_weight.reshape(BLOCK, 1, TILE)
    source_vector = ((BLOCK, 1, TILE), F32)
    target_vector = ((BLOCK, 1, HALF), F32)
    matrix = (BLOCK, TILE, BLOCK * HALF)
    columns = (BLOCK, TILE, LANES)
    hbm = pltpu.HBM

    score, packed, meta, x, y, warm = call(
        first_source_kernel,
        "first_source",
        [
            (matrix, F32),
            ((2 * BLOCK, 1, TILE), F32),
            ((8, LANES), jnp.int32),
            ((BLOCK, TILE, width), bf16),
            ((BLOCK, HALF, width), bf16),
            target_vector,
        ],
        [
            pltpu.SMEM(source_bounds.shape, jnp.int32),
            pltpu.SMEM(target_bounds.shape, jnp.int32),
            pltpu.SMEM(kept_pairs.shape[::-1], jnp.int32),
            pltpu.SemaphoreType.DMA((4,)),
            pltpu.SemaphoreType.DMA((3,)),
        ],
        [
            source_emb.reshape(BLOCK, TILE, width),
            target_emb.reshape(BLOCK, 2, HALF, width),
            warm_start.reshape(BLOCK, 2, 1, HALF),
            source_bounds,
            target_bounds,
            kept_pairs.T,
        ],
        [hbm] * 6,
    )
    parts = spread(packed, over_source)
    n_source = len(parts)
    e, packed = call(
        functools.partial(first_target_kernel, n_source),
        "first_target",
        [(matrix, F32), ((2 * BLOCK, 1, HALF), F32)],
        [pltpu.VMEM(columns, F32)],
        [*parts, score, meta],
    )
    parts = spread(packed, over_target)
    n_target = len(parts)
    sums, q, wq = call(
        functools.partial(second_source_kernel, n_target),
        "second_source",
        [source_vector, target_vector, target_vector],
        [],
        [*parts, warm, e],
    )
    parts = spread(sums, over_source)
    sums, a, a_column = call(
        functools.partial(second_target_kernel, n_source),
        "second_target",
        [target_vector, source_vector, (columns, F32)],
        [],
        [*parts, e, q],
    )
    parts = spread(sums, over_target)
    sums, p = call(
        functools.partial(late_kernel, n_target),
        "late",
        [source_vector, target_vector],
        [],
        [*parts, e, q, target_weight],
    )
    parts = spread(sums, over_source)
    sums, b_column = call(
        functools.partial(mid_kernel, n_source),
        "mid",
        [target_vector, (columns, F32)],
        [],
        [*parts, e, q, a, source_weight],
    )
    parts = spread(sums, over_target)
    sums, h = call(
        functools.partial(early_kernel, n_target),
        "early",
        [source_vector, target_vector],
        [],
        [*parts, e, q],
    )
    parts = spread(sums, over_source)

    rows = sizes["row"]
    per_tile = rows // BLOCK
    piece = HALF // per_tile
    shared = [x, e, a_column, b_column, p, q, h, wq]
    pieces = [None] * rows
    arrived = [None] * rows
    bar = early = None
    for part in (3, 2, 1, 0):
        outs = [((piece, width), bf16 if part or i else F32) for i in range(per_tile)]
        if bar is None:
            bar, early, *results = call(
                functools.partial(target_gradient_kernel, part, n_source),
                f"target_gradient_{part}",
                [(matrix, bf16), (columns, F32)] + outs,
                [],
                [*parts, *shared],
            )
        else:
            if part == 0:
                first = slice((3, 2, 1, 0)[0] * per_tile, ((3, 2, 1, 0)[0] + 1) * per_tile)
                bar, arrived[first] = lax.optimization_barrier((bar, arrived[first]))
            bar, *results = call(
                functools.partial(target_gradient_kernel, part, 0),
                f"target_gradient_{part}",
                [(matrix, bf16)] + outs,
                [],
                [*shared, early, bar],
                aliases={len(shared) + 1: 0},
            )
        for i, value in enumerate(results):
            k = part * per_tile + i
            pieces[k] = value
            arrived[k] = swap(value, over_target, k) if k else value
    source_piece = BLOCK * TILE // n_source
    columns_of_chips = sizes["col"]
    halves = (columns_of_chips, source_piece, width)
    near, far = call(
        source_gradient_kernel,
        "source_gradient",
        [(halves, F32), (halves, bf16)],
        [pltpu.VMEM((BLOCK * TILE, width), F32)],
        [bar, y],
    )
    def added(values):
        value = values[0].astype(F32)
        for other in values[1:]:
            value = value + other.astype(F32)
        return value.astype(bf16)

    arrived, far = lax.optimization_barrier((arrived, far))
    target_rows = added(arrived)
    merged = call(
        merge_kernel,
        "merge",
        [((source_piece, width), bf16 if d else F32) for d in range(columns_of_chips)],
        [],
        [near, swap(far, ("rep",), 1)],
    )
    terms = [merged[0]] + [swap(merged[d], ("col",), d) for d in range(1, columns_of_chips)]
    gathered = spread(target_rows, over_target)
    crossed = [swap(value, ("rep",), 1) for value in gathered]
    late_ones = [k for k in range(rows) if k // per_tile in (1, 2)]
    ranks = [(k, 0) for k in range(rows)]
    ranks += [(k, 1) for k in range(rows) if k not in late_ones]
    source_shape = (source_piece, width)
    on_vmem = pl.BlockSpec(memory_space=pltpu.VMEM)
    on_hbm = pl.BlockSpec(memory_space=pltpu.HBM)
    target_out = jax.ShapeDtypeStruct(target_emb.shape, bf16)
    params = pltpu.CompilerParams(vmem_limit_bytes=LIMIT)
    grad_source, grad_target = pl.pallas_call(
        functools.partial(finish_kernel, ranks, len(terms)),
        name="finish",
        out_shape=[jax.ShapeDtypeStruct(source_shape, bf16), target_out],
        in_specs=[on_vmem] * (len(ranks) + len(terms)),
        out_specs=[on_hbm] * 2,
        scratch_shapes=[
            pltpu.VMEM(source_shape, bf16),
            pltpu.SemaphoreType.DMA((len(ranks) + 1,)),
        ],
        compiler_params=params,
    )(*[(crossed if c else gathered)[k] for k, c in ranks], *terms)
    ranks = [(k, 1) for k in late_ones]
    grad_target = pl.pallas_call(
        functools.partial(finish_kernel, ranks, 0),
        name="finish_last",
        out_shape=target_out,
        in_specs=[on_vmem] * len(ranks) + [on_hbm],
        out_specs=on_hbm,
        scratch_shapes=[pltpu.SemaphoreType.DMA((len(ranks),))],
        input_output_aliases={len(ranks): 0},
        compiler_params=params,
    )(*[crossed[k] for k in late_ones], grad_target)
    return grad_source, grad_target


def solution(mesh):
    return jax.shard_map(
        functools.partial(shards, dict(mesh.shape)),
        mesh=mesh,
        in_specs=(
            P(("groups", "row"), None),
            P(("groups", "col"), None),
            P(("groups", "col")),
            P(("groups", "row")),
            P(("groups", "col")),
            P("groups"),
            P("groups"),
            P("groups", None),
        ),
        out_specs=(P(("groups", "row", "col", "rep"), None), P(("groups", "col"), None)),
        check_vma=False,
    )
```

```python
import functools
import math

import jax
import jax.numpy as jnp
from jax import lax
from jax.experimental import pallas as pl
from jax.experimental.pallas import tpu as pltpu
from jax.sharding import PartitionSpec as P

TILE = 512
HALF = 256
BLOCK = 4
LANES = 128
ROWS = 64
LIMIT = 24 * 1024 * 1024
LOWEST = -1e30
NEAR = 60.0
F32 = jnp.float32
NT_DIMS = (((1,), (1,)), ((), ()))
NN_DIMS = (((1,), (0,)), ((), ()))
TN_DIMS = (((0,), (0,)), ((), ()))


def kept_targets(meta, s):
    first_cut, second_cut, straight = meta
    is_low = (s < first_cut).astype(jnp.int32) == straight
    return jnp.where(is_low, 0, second_cut), jnp.where(is_low, second_cut, BLOCK)


def tile_lanes(t):
    return pl.ds(pl.multiple_of(t * HALF, HALF), HALF)


def to_column(row):
    return jnp.broadcast_to(row, (LANES, row.shape[1])).T


def lane_sums(values):
    return jnp.sum(values.T, axis=0, keepdims=True)


def total(refs, index):
    value = refs[0][index]
    for ref in refs[1:]:
        value = value + ref[index]
    return value


def tile_biases(meta, s):
    low, high = kept_targets(meta, s)
    return [jnp.where((low <= t) & (t < high), 0.0, LOWEST) for t in range(BLOCK)]


def lane_groups():
    return [(i // 2, slice(i * LANES, (i + 1) * LANES)) for i in range(2 * BLOCK)]


def half_of(i):
    return slice((i % 2) * LANES, (i % 2 + 1) * LANES)


def weighted_rows(e_ref, vector_ref, out_ref):
    for s in range(BLOCK):
        for at in range(0, TILE, LANES):
            acc = None
            for i, (t, lanes) in enumerate(lane_groups()):
                term = e_ref[s, at : at + LANES, lanes] * vector_ref[t, :, half_of(i)]
                acc = term if acc is None else acc + term
            out_ref[s, :, at : at + LANES] = lane_sums(acc)


def eight_rows(values, reduce):
    return reduce(values.reshape(-1, 8, LANES), axis=0)


def weighted_columns(e_ref, column_ref, scale_ref, out_ref):
    acc = [None] * (2 * BLOCK)
    for s in range(BLOCK):
        for at in range(0, TILE, LANES):
            u = column_ref[s, at : at + LANES, :]
            for i, (t, lanes) in enumerate(lane_groups()):
                term = eight_rows(e_ref[s, at : at + LANES, lanes] * u, jnp.sum)
                acc[i] = term if acc[i] is None else acc[i] + term
    for i, (t, lanes) in enumerate(lane_groups()):
        half = half_of(i)
        out_ref[t, :, half] = scale_ref[t, :, half] * jnp.sum(acc[i], axis=0, keepdims=True)


def first_source_kernel(
    x_hbm,
    y_hbm,
    warm_hbm,
    sb_hbm,
    tb_hbm,
    kp_hbm,
    score_ref,
    out_ref,
    x_ref,
    y_ref,
    sb_ref,
    tb_ref,
    kp_ref,
    warm_ref,
    sems,
    bound_sems,
):
    row_pos = lax.axis_index("row")
    col_pos = lax.axis_index("col")
    rep_pos = lax.axis_index("rep")
    bounds = [
        pltpu.make_async_copy(source, target, bound_sems.at[i])
        for i, (source, target) in enumerate(
            ((sb_hbm, sb_ref), (tb_hbm, tb_ref), (kp_hbm, kp_ref))
        )
    ]
    y_copy = pltpu.make_async_copy(y_hbm.at[:, rep_pos], y_ref, sems.at[0])
    x_copy = pltpu.make_async_copy(x_hbm.at[:1], x_ref.at[:1], sems.at[1])
    rest_copy = pltpu.make_async_copy(x_hbm.at[1:], x_ref.at[1:], sems.at[2])
    warm_copy = pltpu.make_async_copy(warm_hbm.at[:, rep_pos], warm_ref, sems.at[3])
    copies = [y_copy, x_copy, *bounds, warm_copy, rest_copy]
    for copy in copies:
        copy.start()
    for copy in bounds:
        copy.wait()
    first_cut = sb_ref[2 * row_pos + 1] - BLOCK * row_pos
    second_cut = tb_ref[2 * col_pos + 1] - BLOCK * col_pos

    def look(i, found):
        here = (kp_ref[0, i] == 2 * row_pos) & (kp_ref[1, i] == 2 * col_pos)
        return found | here.astype(jnp.int32)

    straight = lax.fori_loop(0, kp_ref.shape[1], look, jnp.int32(0))
    meta = (first_cut, second_cut, straight)
    width = x_ref.shape[2]
    scale = width ** (-0.5) * math.log2(math.e)

    def scores(s):
        biases = tile_biases(meta, s)
        row = jnp.concatenate(
            [warm_ref[t] * math.log2(math.e) + biases[t] for t in range(BLOCK)], axis=1
        )
        product = lax.dot_general(
            x_ref[s],
            y_ref[...].reshape(BLOCK * HALF, width),
            NT_DIMS,
            preferred_element_type=F32,
        )
        score_ref[s] = scale * product + row

    def passes(s):
        for at in range(0, TILE, LANES):
            largest = None
            for _, lanes in lane_groups():
                term = score_ref[s, at : at + LANES, lanes]
                largest = term if largest is None else jnp.maximum(largest, term)
            largest = jnp.max(largest, axis=1, keepdims=True)
            largest = jnp.broadcast_to(largest, (LANES, LANES))
            acc = None
            for _, lanes in lane_groups():
                term = jnp.exp2(score_ref[s, at : at + LANES, lanes] - largest)
                acc = term if acc is None else acc + term
            out_ref[s, :, at : at + LANES] = largest.T[:1] + jnp.log2(lane_sums(acc))

    warm_copy.wait()
    y_copy.wait()
    x_copy.wait()
    scores(0)
    rest_copy.wait()
    for s in range(BLOCK):
        if s + 1 < BLOCK:
            scores(s + 1)
        passes(s)


def combine(refs, at):
    largest = refs[0][at]
    for ref in refs[1:]:
        largest = jnp.maximum(largest, ref[at])
    sums = jnp.exp2(refs[0][at] - largest)
    for ref in refs[1:]:
        sums = sums + jnp.exp2(ref[at] - largest)
    return -(largest + jnp.log2(sums))


def peaks(score_ref, column_ref, out_ref):
    largest = [None] * (2 * BLOCK)
    for s in range(BLOCK):
        for at in range(0, TILE, LANES):
            u = column_ref[s, at : at + LANES, :]
            for i, (_, lanes) in enumerate(lane_groups()):
                term = eight_rows(score_ref[s, at : at + LANES, lanes] + u, jnp.max)
                largest[i] = term if largest[i] is None else jnp.maximum(largest[i], term)
    for i, (t, _) in enumerate(lane_groups()):
        out_ref[t, :, half_of(i)] = jnp.max(largest[i], axis=0, keepdims=True)


def own_peaks_kernel(own_ref, score_ref, out_ref, column_ref):
    for s in range(BLOCK):
        column_ref[s] = to_column(-own_ref[s])
    peaks(score_ref, column_ref, out_ref)


def first_target_kernel(count, *args):
    parts = args[:count]
    score_ref, own_peaks_ref, e_ref, out_ref, shift_ref, column_ref = args[count:]
    gap = None
    for s in range(BLOCK):
        potential = combine(parts, s)
        column_ref[s] = to_column(potential)
        term = -potential - parts[0][s]
        gap = term if gap is None else jnp.maximum(gap, term)
    is_near = jnp.max(gap) <= NEAR

    @pl.when(is_near)
    def _():
        shift_ref[...] = own_peaks_ref[...]

    @pl.when(jnp.logical_not(is_near))
    def _():
        peaks(score_ref, column_ref, shift_ref)

    sums = [None] * (2 * BLOCK)
    shifts = [shift_ref[t, :, half_of(i)] for i, (t, _) in enumerate(lane_groups())]
    for s in range(BLOCK):
        for at in range(0, TILE, LANES):
            u = column_ref[s, at : at + LANES, :]
            for i, (_, lanes) in enumerate(lane_groups()):
                e = jnp.exp2(score_ref[s, at : at + LANES, lanes] + u - shifts[i])
                e_ref[s, at : at + LANES, lanes] = e
                term = eight_rows(e, jnp.sum)
                sums[i] = term if sums[i] is None else sums[i] + term
    for i, (t, _) in enumerate(lane_groups()):
        value = jnp.sum(sums[i], axis=0, keepdims=True)
        out_ref[t, :, half_of(i)] = shifts[i] + jnp.log2(value)


def second_source_kernel(count, *args):
    parts = args[:count]
    shift_ref, e_ref, out_ref, q_ref, wq_ref = args[count:]
    for t in range(BLOCK):
        potential = combine(parts, t)
        q = jnp.exp2(shift_ref[t] + potential)
        q_ref[t] = q
        wq_ref[t] = q * jnp.exp2(-potential)
    weighted_rows(e_ref, q_ref, out_ref)


def second_target_kernel(count, *args):
    parts = args[:count]
    e_ref, q_ref, out_ref, a_ref, column_ref = args[count:]
    for s in range(BLOCK):
        a = 1.0 / total(parts, s)
        a_ref[s] = a
        column_ref[s] = to_column(a)
    weighted_columns(e_ref, column_ref, q_ref, out_ref)


def late_kernel(count, *args):
    parts = args[:count]
    e_ref, q_ref, weight_ref, out_ref, p_ref = args[count:]
    rep_pos = lax.axis_index("rep")
    for t in range(BLOCK):
        p_ref[t] = weight_ref[2 * t + rep_pos] * q_ref[t] / total(parts, t)
    weighted_rows(e_ref, p_ref, out_ref)


def mid_kernel(count, *args):
    parts = args[:count]
    e_ref, q_ref, a_ref, weight_ref, out_ref, column_ref = args[count:]
    for s in range(BLOCK):
        a = a_ref[s]
        column_ref[s] = to_column(a * (weight_ref[s] - a * total(parts, s)))
    weighted_columns(e_ref, column_ref, q_ref, out_ref)


def early_kernel(count, *args):
    parts = args[:count]
    e_ref, q_ref, out_ref, h_ref = args[count:]
    for t in range(BLOCK):
        h_ref[t] = -q_ref[t] * total(parts, t)
    weighted_rows(e_ref, h_ref, out_ref)


def target_gradient_kernel(part, count, *args):
    if count:
        parts = args[:count]
        x_ref, e_ref, a_ref, b_ref, p_ref, q_ref, h_ref, wq_ref = args[count : count + 8]
        bar_ref, early_ref, *out_refs = args[count + 8 :]
        for s in range(BLOCK):
            early_ref[s] = to_column(-total(parts, s))
    else:
        x_ref, e_ref, a_ref, b_ref, p_ref, q_ref, h_ref, wq_ref = args[:8]
        early_ref, _, bar_ref, *out_refs = args[8:]
    row_pos = lax.axis_index("row")
    per_tile = len(out_refs)
    t = (row_pos // per_tile) ^ part
    p, q, h, wq = p_ref[t], q_ref[t], h_ref[t], wq_ref[t]
    width = x_ref.shape[2]
    result = None
    for s in range(BLOCK):
        bars = []
        for at in range(0, TILE, ROWS):
            e = e_ref[s, at : at + ROWS, tile_lanes(t)]
            a = a_ref[s, at : at + ROWS, :]
            b = b_ref[s, at : at + ROWS, :]
            early = early_ref[s, at : at + ROWS, :]
            sides = []
            for side in (slice(0, LANES), slice(LANES, HALF)):
                factor = a * p[:, side] + b * q[:, side] + (h[:, side] + early * wq[:, side])
                sides.append((e[:, side] * factor).astype(jnp.bfloat16))
            bars.append(jnp.concatenate(sides, axis=1))
        bar = jnp.concatenate(bars, axis=0)
        bar_ref[s, :, tile_lanes(t)] = bar
        term = lax.dot_general(bar, x_ref[s], TN_DIMS, preferred_element_type=F32)
        result = term if result is None else result + term
    result = -(width ** (-0.5)) * result
    if per_tile == 1:
        out_refs[0][...] = result.astype(out_refs[0].dtype)
        return
    piece = HALF // per_tile
    for i, ref in enumerate(out_refs):
        for j in range(per_tile):

            @pl.when(((row_pos % per_tile) ^ i) == j)
            def _():
                ref[...] = result[j * piece : (j + 1) * piece, :].astype(ref.dtype)


def source_gradient_kernel(bar_ref, y_ref, near_ref, far_ref, acc_ref):
    width = y_ref.shape[2]
    col_pos = lax.axis_index("col")
    rep_pos = lax.axis_index("rep")
    y = y_ref[...].reshape(BLOCK * HALF, width)
    for s in range(BLOCK):
        acc_ref[s * TILE : (s + 1) * TILE, :] = -(width ** (-0.5)) * lax.dot_general(
            bar_ref[s], y, NN_DIMS, preferred_element_type=F32
        )
    piece = near_ref.shape[1]
    for d in range(near_ref.shape[0]):
        at = 2 * (col_pos ^ d)
        for ref, rep in ((near_ref, rep_pos), (far_ref, 1 - rep_pos)):
            begin = pl.multiple_of((at + rep) * piece, piece)
            ref[d] = acc_ref[pl.ds(begin, piece), :].astype(ref.dtype)


def merge_kernel(near_ref, far_ref, *out_refs):
    for d, ref in enumerate(out_refs):
        ref[...] = (near_ref[d] + far_ref[d].astype(F32)).astype(ref.dtype)


def finish_kernel(ranks, count, *args):
    pieces, args = args[: len(ranks)], args[len(ranks) :]
    terms, args = args[:count], args[count:]
    if terms:
        source_out, target_out, sum_ref, sems = args
    else:
        _, target_out, sems = args
    rep_pos = lax.axis_index("rep")
    row_pos = lax.axis_index("row")
    piece = pieces[0].shape[0]
    per_tile = HALF // piece
    copies = []
    for i, ((k, crossed), ref) in enumerate(zip(ranks, pieces)):
        at = row_pos ^ k
        rep = 1 - rep_pos if crossed else rep_pos
        begin = (at // per_tile) * TILE + rep * HALF + (at % per_tile) * piece
        begin = pl.multiple_of(begin, piece)
        copies.append(
            pltpu.make_async_copy(ref, target_out.at[pl.ds(begin, piece)], sems.at[i])
        )
    for copy in copies:
        copy.start()
    if terms:
        value = terms[0][...]
        for term in terms[1:]:
            value = value + term[...].astype(F32)
        sum_ref[...] = value.astype(sum_ref.dtype)
        copies.append(pltpu.make_async_copy(sum_ref, source_out, sems.at[len(ranks)]))
        copies[-1].start()
    for copy in copies:
        copy.wait()


def call(kernel, name, outs, scratch, args, spaces=None, aliases=None, cost=None):
    spaces = spaces or [pltpu.VMEM] * len(args)
    args = [
        pltpu.with_memory_space_constraint(value, space)
        for value, space in zip(args, spaces)
    ]
    return pl.pallas_call(
        kernel,
        name=name,
        out_shape=[pltpu.VMEM(shape, dtype) for shape, dtype in outs],
        in_specs=[pl.BlockSpec(memory_space=space) for space in spaces],
        out_specs=[pl.BlockSpec(memory_space=pltpu.VMEM) for _ in outs],
        scratch_shapes=scratch,
        input_output_aliases=aliases or {},
        cost_estimate=cost,
        compiler_params=pltpu.CompilerParams(vmem_limit_bytes=LIMIT),
    )(*args)


def shards(
    sizes,
    source_emb,
    target_emb,
    warm_start,
    source_weight,
    target_weight,
    source_bounds,
    target_bounds,
    kept_pairs,
):
    width = source_emb.shape[1]

    def swap(value, axes, k):
        count = math.prod(sizes[axis] for axis in axes)
        return lax.ppermute(value, axes, [(i, i ^ k) for i in range(count)])

    def spread(value, axes):
        count = math.prod(sizes[axis] for axis in axes)
        order = list(range(1, count))
        if "rep" not in axes:
            order.sort(key=lambda k: (k % 4 == 2, k))
        return [value] + [swap(value, axes, k) for k in order]

    bf16 = jnp.bfloat16
    over_source = ("col", "rep")
    over_target = ("row",)
    target_weight = target_weight.reshape(2 * BLOCK, 1, HALF)
    source_weight = source_weight.reshape(BLOCK, 1, TILE)
    source_vector = ((BLOCK, 1, TILE), F32)
    target_vector = ((BLOCK, 1, HALF), F32)
    matrix = (BLOCK, TILE, BLOCK * HALF)
    columns = (BLOCK, TILE, LANES)
    hbm = pltpu.HBM

    score, sums, x, y = call(
        first_source_kernel,
        "first_source",
        [
            (matrix, F32),
            source_vector,
            ((BLOCK, TILE, width), bf16),
            ((BLOCK, HALF, width), bf16),
        ],
        [
            pltpu.SMEM(source_bounds.shape, jnp.int32),
            pltpu.SMEM(target_bounds.shape, jnp.int32),
            pltpu.SMEM(kept_pairs.shape[::-1], jnp.int32),
            pltpu.VMEM(target_vector[0], F32),
            pltpu.SemaphoreType.DMA((4,)),
            pltpu.SemaphoreType.DMA((3,)),
        ],
        [
            source_emb.reshape(BLOCK, TILE, width),
            target_emb.reshape(BLOCK, 2, HALF, width),
            warm_start.reshape(BLOCK, 2, 1, HALF),
            source_bounds,
            target_bounds,
            kept_pairs.T,
        ],
        [hbm] * 6,
    )
    parts = spread(sums, over_source)
    n_source = len(parts)
    (own_peaks,) = call(
        own_peaks_kernel,
        "own_peaks",
        [target_vector],
        [pltpu.VMEM(columns, F32)],
        [sums, score],
    )
    e, sums, shift = call(
        functools.partial(first_target_kernel, n_source),
        "first_target",
        [(matrix, F32), target_vector, target_vector],
        [pltpu.VMEM(columns, F32)],
        [*parts, score, own_peaks],
    )
    parts = spread(sums, over_target)
    n_target = len(parts)
    sums, q, wq = call(
        functools.partial(second_source_kernel, n_target),
        "second_source",
        [source_vector, target_vector, target_vector],
        [],
        [*parts, shift, e],
    )
    parts = spread(sums, over_source)
    sums, a, a_column = call(
        functools.partial(second_target_kernel, n_source),
        "second_target",
        [target_vector, source_vector, (columns, F32)],
        [],
        [*parts, e, q],
    )
    parts = spread(sums, over_target)
    sums, p = call(
        functools.partial(late_kernel, n_target),
        "late",
        [source_vector, target_vector],
        [],
        [*parts, e, q, target_weight],
    )
    parts = spread(sums, over_source)
    sums, b_column = call(
        functools.partial(mid_kernel, n_source),
        "mid",
        [target_vector, (columns, F32)],
        [],
        [*parts, e, q, a, source_weight],
    )
    parts = spread(sums, over_target)
    sums, h = call(
        functools.partial(early_kernel, n_target),
        "early",
        [source_vector, target_vector],
        [],
        [*parts, e, q],
    )
    parts = spread(sums, over_source)

    rows = sizes["row"]
    per_tile = rows // BLOCK
    piece = HALF // per_tile
    shared = [x, e, a_column, b_column, p, q, h, wq]
    pieces = [None] * rows
    arrived = [None] * rows
    bar = early = None
    for part in (3, 2, 1, 0):
        outs = [((piece, width), bf16 if part or i else F32) for i in range(per_tile)]
        if bar is None:
            bar, early, *results = call(
                functools.partial(target_gradient_kernel, part, n_source),
                f"target_gradient_{part}",
                [(matrix, bf16), (columns, F32)] + outs,
                [],
                [*parts, *shared],
            )
        else:
            if part == 0:
                first = slice((3, 2, 1, 0)[0] * per_tile, ((3, 2, 1, 0)[0] + 1) * per_tile)
                bar, arrived[first] = lax.optimization_barrier((bar, arrived[first]))
            bar, *results = call(
                functools.partial(target_gradient_kernel, part, 0),
                f"target_gradient_{part}",
                [(matrix, bf16)] + outs,
                [],
                [*shared, early, bar],
                aliases={len(shared) + 1: 0},
            )
        for i, value in enumerate(results):
            k = part * per_tile + i
            pieces[k] = value
            arrived[k] = swap(value, over_target, k) if k else value
    source_piece = BLOCK * TILE // n_source
    columns_of_chips = sizes["col"]
    halves = (columns_of_chips, source_piece, width)
    near, far = call(
        source_gradient_kernel,
        "source_gradient",
        [(halves, F32), (halves, bf16)],
        [pltpu.VMEM((BLOCK * TILE, width), F32)],
        [bar, y],
    )
    def added(values):
        value = values[0].astype(F32)
        for other in values[1:]:
            value = value + other.astype(F32)
        return value.astype(bf16)

    arrived, far = lax.optimization_barrier((arrived, far))
    target_rows = added(arrived)
    merged = call(
        merge_kernel,
        "merge",
        [((source_piece, width), bf16 if d else F32) for d in range(columns_of_chips)],
        [],
        [near, swap(far, ("rep",), 1)],
    )
    terms = [merged[0]] + [swap(merged[d], ("col",), d) for d in range(1, columns_of_chips)]
    gathered = [swap(target_rows, over_target, k) if k else target_rows for k in range(rows)]
    crossed = [swap(value, ("rep",), 1) for value in gathered]
    late_ones = [k for k in range(rows) if k // per_tile in (1, 2)]
    ranks = [(k, 0) for k in range(rows)]
    ranks += [(k, 1) for k in range(rows) if k not in late_ones]
    source_shape = (source_piece, width)
    on_vmem = pl.BlockSpec(memory_space=pltpu.VMEM)
    on_hbm = pl.BlockSpec(memory_space=pltpu.HBM)
    target_out = jax.ShapeDtypeStruct(target_emb.shape, bf16)
    params = pltpu.CompilerParams(vmem_limit_bytes=LIMIT)
    grad_source, grad_target = pl.pallas_call(
        functools.partial(finish_kernel, ranks, len(terms)),
        name="finish",
        out_shape=[jax.ShapeDtypeStruct(source_shape, bf16), target_out],
        in_specs=[on_vmem] * (len(ranks) + len(terms)),
        out_specs=[on_hbm] * 2,
        scratch_shapes=[
            pltpu.VMEM(source_shape, bf16),
            pltpu.SemaphoreType.DMA((len(ranks) + 1,)),
        ],
        compiler_params=params,
    )(*[(crossed if c else gathered)[k] for k, c in ranks], *terms)
    ranks = [(k, 1) for k in late_ones]
    grad_target = pl.pallas_call(
        functools.partial(finish_kernel, ranks, 0),
        name="finish_last",
        out_shape=target_out,
        in_specs=[on_vmem] * len(ranks) + [on_hbm],
        out_specs=on_hbm,
        scratch_shapes=[pltpu.SemaphoreType.DMA((len(ranks),))],
        input_output_aliases={len(ranks): 0},
        compiler_params=params,
    )(*[crossed[k] for k in late_ones], grad_target)
    return grad_source, grad_target


def solution(mesh):
    return jax.shard_map(
        functools.partial(shards, dict(mesh.shape)),
        mesh=mesh,
        in_specs=(
            P(("groups", "row"), None),
            P(("groups", "col"), None),
            P(("groups", "col")),
            P(("groups", "row")),
            P(("groups", "col")),
            P("groups"),
            P("groups"),
            P("groups", None),
        ),
        out_specs=(P(("groups", "row", "col", "rep"), None), P(("groups", "col"), None)),
        check_vma=False,
    )
```
